32 devices in a mesh: ctx: 4 (over y, core), grp: 8 (over z, x).
Axes of the slice: x: 2, y: 2, z: 4, core: 2. Of those that a mesh axis runs over, the one named last changes fastest.
Arguments:
- query_feat: bfloat16 [8192, 4096], P(('ctx', 'grp')), may hold values from 0.0099487305 to 1
- key_feat: bfloat16 [8192, 4096], P(('ctx', 'grp')), may hold values from 0.0099487305 to 1
- values: bfloat16 [8192, 2048], P(('ctx', 'grp')), may hold values from -6 to 6
- teacher: bfloat16 [8192, 2048], P('ctx', 'grp'), may hold values from -4 to 4
Outputs:
- query_grad: bfloat16 [8192, 4096], P(('ctx', 'grp'))
- key_grad: bfloat16 [8192, 4096], P(('ctx', 'grp'))
The draws below stay inside these ranges and needn't reach their ends.
All inputs are finite; a program needn't handle non-finite values.
Results may differ from the reference program's by a relative error of at most 0.001.
Values may be sent and summed in bfloat16 or wider, within the bound.
A program may use at most 576 MiB of HBM per device.

```python
import math
import jax
import jax.numpy as jnp
from jax import lax

H = 16
DH = 128
FEAT = 256
TOKENS = 8192


def block_scale(own_key, extent, shards, least, top_value):
    def one(dim, shards_of):
        draws = jax.random.uniform(jax.random.fold_in(jax.random.fold_in(own_key, 6), dim), (shards_of,), jnp.float32, least / len(shards), top_value / len(shards))
        return jnp.repeat(jnp.exp(draws), extent[dim] // shards_of).reshape((-1,) + (1,) * (len(extent) - dim - 1))

    gain = one(*shards[0])
    for cut in shards[1:]:
        gain = gain * one(*cut)
    return gain


def scatter_about(key, dims, scale, reach, cuts=(), kind=jnp.bfloat16):
    array = jax.random.normal(key, dims, jnp.float32) * scale
    if len(cuts) > 0:
        array = block_scale(key, dims, cuts, -0.22, 0.18) * array
    return jnp.clip(array, min=-reach, max=reach).astype(kind)


def setup_inputs(seed: int = 0) -> dict:
    splits = jax.random.split(jax.random.key(seed), 5)
    query_feat = jnp.clip(jnp.exp(math.log(1.0) - 4.61031033 * jax.random.uniform(splits[0], (TOKENS, H * FEAT), jnp.float32) ** block_scale(splits[0], (TOKENS, H * FEAT), ((0, 32),), -0.2, 0.2)), 0.0099487305, 1.0).astype(jnp.bfloat16)
    key_feat = jnp.clip(jnp.exp(math.log(1.0) - 4.61031033 * jax.random.uniform(splits[1], (TOKENS, H * FEAT), jnp.float32) ** block_scale(splits[1], (TOKENS, H * FEAT), ((0, 32),), -0.2, 0.2)), 0.0099487305, 1.0).astype(jnp.bfloat16)
    values = scatter_about(splits[2], (TOKENS, H * DH), 1.0, 6.0, ((0, 32),))
    teacher = scatter_about(splits[3], (TOKENS, H * DH), 0.5, 4.0, ((0, 4), (1, 8)))
    return dict(query_feat=query_feat, key_feat=key_feat, values=values, teacher=teacher)


HIGH = lax.Precision.HIGHEST


def one_head(query_one, key_one, value_one, teacher_one, block):
    count = query_one.shape[0] // block
    feat = query_one.shape[1]
    width = value_one.shape[1]
    qs = query_one.reshape(count, block, feat)
    ks = key_one.reshape(count, block, feat)
    vs = value_one.reshape(count, block, width)
    ys = teacher_one.reshape(count, block, width)
    rows_t = lax.broadcasted_iota(jnp.int32, (block, block), 0)
    rows_s = lax.broadcasted_iota(jnp.int32, (block, block), 1)
    causal = (rows_s <= rows_t).astype(jnp.float32)

    def forward(carry, piece):
        kv_now, key_now = carry
        q, k, v, y = piece
        scores = jnp.dot(q, k.T, precision=HIGH) * causal
        numer = jnp.dot(scores, v, precision=HIGH) + jnp.dot(q, kv_now, precision=HIGH)
        denom = jnp.sum(scores, axis=1) + jnp.dot(q, key_now, precision=HIGH)
        student = numer / denom[:, None]
        resid = student - y
        d_numer = resid / denom[:, None]
        d_denom = -jnp.sum(resid * student, axis=1) / denom
        mixed = (jnp.dot(d_numer, v.T, precision=HIGH) + d_denom[:, None]) * causal
        q_grad = jnp.dot(mixed, k, precision=HIGH) + jnp.dot(d_numer, kv_now.T, precision=HIGH) + d_denom[:, None] * key_now[None, :]
        new_carry = (kv_now + jnp.dot(k.T, v, precision=HIGH), key_now + jnp.sum(k, axis=0))
        return new_carry, (q_grad, d_numer, d_denom)

    start = (jnp.zeros((feat, width), jnp.float32), jnp.zeros((feat,), jnp.float32))
    unused, (q_grads, d_numers, d_denoms) = lax.scan(forward, start, (qs, ks, vs, ys))

    def backward(carry, piece):
        after_kv, after_q = carry
        q, k, v, d_numer, d_denom = piece
        mixed = (jnp.dot(d_numer, v.T, precision=HIGH) + d_denom[:, None]) * causal
        k_grad = jnp.dot(mixed.T, q, precision=HIGH) + jnp.dot(v, after_kv.T, precision=HIGH) + after_q[None, :]
        new_carry = (after_kv + jnp.dot(q.T, d_numer, precision=HIGH), after_q + jnp.dot(d_denom, q, precision=HIGH))
        return new_carry, k_grad

    unused_two, k_grads = lax.scan(backward, start, (qs, ks, vs, d_numers, d_denoms), reverse=True)
    return q_grads.reshape(-1, feat), k_grads.reshape(-1, feat)


def reference(query_feat, key_feat, values, teacher):
    block = math.gcd(TOKENS, 512)
    scale = float(TOKENS) ** 0.5
    query3 = query_feat.reshape(TOKENS, H, FEAT)
    key3 = key_feat.reshape(TOKENS, H, FEAT)
    value3 = values.reshape(TOKENS, H, DH)
    teacher3 = teacher.reshape(TOKENS, H, DH)

    def per_head(head):
        query_one = lax.dynamic_index_in_dim(query3, head, 1, False).astype(jnp.float32)
        key_one = lax.dynamic_index_in_dim(key3, head, 1, False).astype(jnp.float32)
        value_one = lax.dynamic_index_in_dim(value3, head, 1, False).astype(jnp.float32)
        teacher_one = lax.dynamic_index_in_dim(teacher3, head, 1, False).astype(jnp.float32)
        q_grad, k_grad = one_head(query_one, key_one, value_one, teacher_one, block)
        return (scale * q_grad).astype(jnp.bfloat16), (scale * k_grad).astype(jnp.bfloat16)

    q_all, k_all = lax.map(per_head, jnp.arange(H, dtype=jnp.int32))
    query_grad = jnp.transpose(q_all, (1, 0, 2)).reshape(TOKENS, H * FEAT)
    key_grad = jnp.transpose(k_all, (1, 0, 2)).reshape(TOKENS, H * FEAT)
    return query_grad, key_grad
```

```python
import functools
import math

import jax
import jax.numpy as jnp
from jax import lax
from jax.experimental import pallas as pl
from jax.experimental.pallas import tpu as pltpu
from jax.sharding import PartitionSpec as P

H = 16
SIDE = 16
SPAN = 125.0
F32 = jnp.float32
BF16 = jnp.bfloat16


def dot(a, b, dims):
    return lax.dot_general(a, b, (dims, ((), ())), preferred_element_type=F32)


NN = ((1,), (0,))
NT = ((1,), (1,))
TN = ((0,), (0,))


def split(x):
    hi = x.astype(BF16)
    return hi, (x - hi.astype(F32)).astype(BF16)


def encode(x):
    scale = (jnp.maximum(jnp.max(jnp.abs(x), axis=0, keepdims=True), 1e-20) * 1.01).astype(BF16)
    y = jnp.exp2(jnp.abs(x) * (2 * SPAN / scale.astype(F32)) - SPAN)
    return jnp.where(x < 0, -y, y).astype(BF16), scale


def decode(code, scale):
    y = code.astype(F32)
    x = (jnp.log2(jnp.abs(y)) + SPAN) * (scale.astype(F32) * (0.5 / SPAN))
    return jnp.where(y < 0, -x, x)


def side_rows(scale, row2):
    hi = row2.astype(BF16).astype(F32)
    mid = (row2 - hi).astype(BF16).astype(F32)
    low = row2 - hi - mid
    pad = jnp.zeros((SIDE - 7, row2.shape[1]), F32)
    return jnp.concatenate([scale.astype(F32), hi, mid, low, pad], axis=0).astype(BF16)


def read_side(side):
    s = side.astype(F32)
    return s[0:1], s[1:3] + s[3:5] + s[5:7]


def write_state(out_ref, state, row):
    pieces, rows = out_ref.shape[0], out_ref.shape[1] - SIDE
    code, scale = encode(state)
    width = state.shape[1]
    row2 = jnp.concatenate([row[:, :width], row[:, width:]], axis=0)
    side = side_rows(scale, row2)
    for p in range(pieces):
        out_ref[p, :rows, :] = code[p * rows : (p + 1) * rows]
        out_ref[p, rows:, :] = side


def read_state(ref):
    pieces, rows = ref.shape[0], ref.shape[1] - SIDE
    parts = []
    for p in range(pieces):
        scale, row2 = read_side(ref[p, rows:, :])
        parts.append(decode(ref[p, :rows, :], scale))
    row = jnp.concatenate([row2[0:1], row2[1:2]], axis=1)
    return jnp.concatenate(parts, axis=0), row


def local_kernel(k_ref, v_ref, out_ref):
    k = k_ref[...]
    write_state(out_ref, dot(k, v_ref[...], TN), jnp.sum(k.astype(F32), axis=0, keepdims=True))


def scan_kernel(reverse, in_ref, out_ref):
    n, rows = in_ref.shape[0], in_ref.shape[1] - SIDE

    def step(i, carry):
        state, row2 = carry
        d = n - 1 - i if reverse else i
        code, scale = encode(state)
        out_ref[d, :rows, :] = code
        out_ref[d, rows:, :] = side_rows(scale, row2)
        scale_in, row_in = read_side(in_ref[d, rows:, :])
        return state + decode(in_ref[d, :rows, :], scale_in), row2 + row_in

    width = in_ref.shape[2]
    lax.fori_loop(0, n, step, (jnp.zeros((rows, width), F32), jnp.zeros((2, width), F32)))


def forward_kernel(scale, q_ref, k_ref, v_ref, t_ref, before_ref, qg_ref, kl_ref, adj_ref):
    q, k, v = q_ref[...], k_ref[...], v_ref[...]
    kv, key_row = read_state(before_ref)
    kv_hi, kv_lo = split(kv)
    rows = q.shape[0]
    causal = lax.broadcasted_iota(jnp.int32, (rows, rows), 1) <= lax.broadcasted_iota(
        jnp.int32, (rows, rows), 0
    )
    q_wide = q.astype(F32)
    scores = jnp.where(causal, dot(q, k, NT), 0.0)
    s_hi, s_lo = split(scores)
    numer = dot(s_hi, v, NN) + dot(s_lo, v, NN) + dot(q, kv_hi, NN) + dot(q, kv_lo, NN)
    denom = jnp.sum(scores, axis=1, keepdims=True) + jnp.sum(q_wide * key_row, axis=1, keepdims=True)
    inv = 1.0 / denom
    student = numer * inv
    resid = student - t_ref[...].astype(F32)
    d_numer = resid * inv
    d_denom = -jnp.sum(resid * student, axis=1, keepdims=True) * inv
    dn_hi, dn_lo = split(d_numer)
    adj = dot(q, dn_hi, TN) + dot(q, dn_lo, TN)
    write_state(adj_ref, adj, jnp.sum(d_denom * q_wide, axis=0, keepdims=True))
    mixed = jnp.where(causal, dot(dn_hi, v, NT) + dot(dn_lo, v, NT) + d_denom, 0.0)
    m_hi, m_lo = split(mixed)
    q_grad = dot(m_hi, k, NN) + dot(m_lo, k, NN)
    q_grad = q_grad + dot(dn_hi, kv_hi, NT) + dot(dn_hi, kv_lo, NT) + dot(dn_lo, kv_hi, NT)
    q_grad = q_grad + d_denom * key_row
    qg_ref[...] = (scale * q_grad).astype(BF16)
    kl_ref[...] = dot(m_hi, q, TN) + dot(m_lo, q, TN)


def backward_kernel(scale, v_ref, kl_ref, after_ref, kg_ref):
    adj, row = read_state(after_ref)
    a_hi, a_lo = split(adj)
    v = v_ref[...]
    k_grad = kl_ref[...] + dot(v, a_hi, NT) + dot(v, a_lo, NT) + row
    kg_ref[...] = (scale * k_grad).astype(BF16)


def on_device(n, query_feat, key_feat, values, teacher):
    rows = query_feat.shape[0]
    feat = query_feat.shape[1] // H
    width = values.shape[1] // H
    scale = float(rows * n) ** 0.5
    share = H * feat // n
    per_head = feat // share
    everyone = ("ctx", "grp")
    params = pltpu.CompilerParams(vmem_limit_bytes=32 * 1024 * 1024)

    def cols(w):
        return pl.BlockSpec((rows, w), lambda h: (0, h))

    state_spec = pl.BlockSpec((per_head, share + SIDE, width), lambda h: (h, 0, 0))
    state_shape = jax.ShapeDtypeStruct((n, share + SIDE, width), BF16)

    def swap(x):
        return lax.all_to_all(x, everyone, split_axis=0, concat_axis=0, tiled=True)

    def scan(x, reverse):
        return pl.pallas_call(
            functools.partial(scan_kernel, reverse),
            out_shape=state_shape,
            compiler_params=params,
            name="scan",
        )(x)

    local = pl.pallas_call(
        local_kernel,
        grid=(H,),
        in_specs=[cols(feat), cols(width)],
        out_specs=state_spec,
        out_shape=state_shape,
        compiler_params=params,
        name="local_state",
    )(key_feat, values)
    before = swap(scan(swap(local), False))
    target = lax.all_to_all(teacher, "grp", split_axis=0, concat_axis=1, tiled=True)
    query_grad, key_local, adj = pl.pallas_call(
        functools.partial(forward_kernel, scale),
        grid=(H,),
        in_specs=[cols(feat), cols(feat), cols(width), cols(width), state_spec],
        out_specs=[cols(feat), cols(feat), state_spec],
        out_shape=[
            jax.ShapeDtypeStruct((rows, H * feat), BF16),
            jax.ShapeDtypeStruct((rows, H * feat), F32),
            state_shape,
        ],
        compiler_params=params,
        name="forward",
    )(query_feat, key_feat, values, target, before)
    after = swap(scan(swap(adj), True))
    key_grad = pl.pallas_call(
        functools.partial(backward_kernel, scale),
        grid=(H,),
        in_specs=[cols(width), cols(feat), state_spec],
        out_specs=cols(feat),
        out_shape=jax.ShapeDtypeStruct((rows, H * feat), BF16),
        compiler_params=params,
        name="backward",
    )(values, key_local, after)
    return query_grad, key_grad


def solution(mesh):
    placed = (
        P(("ctx", "grp"), None),
        P(("ctx", "grp"), None),
        P(("ctx", "grp"), None),
        P("ctx", "grp"),
    )
    return jax.shard_map(
        functools.partial(on_device, math.prod(mesh.shape.values())),
        mesh=mesh,
        in_specs=placed,
        out_specs=(P(("ctx", "grp"), None), P(("ctx", "grp"), None)),
        check_vma=False,
    )
```

```python
import functools

import jax
import jax.numpy as jnp
from jax import lax
from jax.experimental import pallas as pl
from jax.experimental.pallas import tpu as pltpu
from jax.sharding import PartitionSpec as P

H = 16
SIDE = 16
SPAN = 125.0
F32 = jnp.float32
BF16 = jnp.bfloat16


def dot(a, b, dims):
    return lax.dot_general(a, b, (dims, ((), ())), preferred_element_type=F32)


NN = ((1,), (0,))
NT = ((1,), (1,))
TN = ((0,), (0,))


def split(x):
    hi = x.astype(BF16)
    return hi, (x - hi.astype(F32)).astype(BF16)


def encode(x):
    scale = (jnp.maximum(jnp.max(jnp.abs(x), axis=0, keepdims=True), 1e-20) * 1.01).astype(BF16)
    y = jnp.exp2(jnp.abs(x) * (2 * SPAN / scale.astype(F32)) - SPAN)
    return jnp.where(x < 0, -y, y).astype(BF16), scale


def decode(code, scale):
    y = code.astype(F32)
    x = (jnp.log2(jnp.abs(y)) + SPAN) * (scale.astype(F32) * (0.5 / SPAN))
    return jnp.where(y < 0, -x, x)


def side_rows(scale, row2):
    hi = row2.astype(BF16).astype(F32)
    mid = (row2 - hi).astype(BF16).astype(F32)
    low = row2 - hi - mid
    pad = jnp.zeros((SIDE - 7, row2.shape[1]), F32)
    return jnp.concatenate([scale.astype(F32), hi, mid, low, pad], axis=0).astype(BF16)


def read_side(side):
    s = side.astype(F32)
    return s[0:1], s[1:3] + s[3:5] + s[5:7]


def write_state(out_ref, state, row):
    pieces, rows = out_ref.shape[0], out_ref.shape[1] - SIDE
    code, scale = encode(state)
    width = state.shape[1]
    row2 = jnp.concatenate([row[:, :width], row[:, width:]], axis=0)
    side = side_rows(scale, row2)
    for p in range(pieces):
        out_ref[p, :rows, :] = code[p * rows : (p + 1) * rows]
        out_ref[p, rows:, :] = side


def read_state(ref):
    pieces, rows = ref.shape[0], ref.shape[1] - SIDE
    parts = []
    for p in range(pieces):
        scale, row2 = read_side(ref[p, rows:, :])
        parts.append(decode(ref[p, :rows, :], scale))
    row = jnp.concatenate([row2[0:1], row2[1:2]], axis=1)
    return jnp.concatenate(parts, axis=0), row


def local_kernel(k_ref, v_ref, out_ref):
    k = k_ref[...]
    write_state(out_ref, dot(k, v_ref[...], TN), jnp.sum(k.astype(F32), axis=0, keepdims=True))


def exchange_kernel(reverse, spans, depth, *refs):
    if reverse:
        in_ref, out_ref = refs[:2]
        scratch = refs[2:]
        teacher_ref = target_ref = None
    else:
        in_ref, teacher_ref, out_ref, target_ref = refs[:4]
        scratch = refs[4:]
    (stage, back, up_out, up_in, down_out, down_in, total, above, below, total_row, above_row,
     below_row, a_send, a_recv, b_send, b_recv, u_send, u_recv, d_send, d_recv, *more) = scratch
    plane = 2 * spans
    chunks, rows = stage.shape[0], stage.shape[2] - SIDE
    ctx, grp = lax.axis_index("ctx"), lax.axis_index("grp")
    groups = 2 * depth
    level, side_x = grp // 2, grp % 2
    mine = ctx * 2 + side_x

    def plane_peer(q):
        return (q // 2, level * 2 + q % 2)

    def remote(src, dst, send, recv, to):
        return pltpu.make_async_remote_copy(
            src_ref=src, dst_ref=dst, send_sem=send, recv_sem=recv, device_id=to,
            device_id_type=pl.DeviceIdType.MESH,
        )

    barrier = pltpu.get_barrier_semaphore()

    def greet(to):
        pl.semaphore_signal(barrier, inc=1, device_id=to, device_id_type=pl.DeviceIdType.MESH)

    for d in range(1, plane):
        greet(plane_peer((mine + d) % plane))
    for d in range(1, groups):
        greet((ctx, (grp + d) % groups))
    pl.semaphore_wait(barrier, plane + groups - 2)

    def gather(j, d):
        peer = (mine + d) % plane
        return remote(in_ref.at[peer * chunks + j], stage.at[j, mine], a_send.at[j, d - 1],
                      a_recv.at[j, d - 1], plane_peer(peer))

    def scatter(j, d):
        peer = (mine + d) % plane
        return remote(back.at[j, peer], out_ref.at[mine * chunks + j], b_send.at[j, d - 1],
                      b_recv.at[j, d - 1], plane_peer(peer))

    def upward(j):
        return remote(up_out.at[j], up_in.at[j], u_send.at[j], u_recv.at[j], (ctx, grp + 2))

    def downward(j):
        return remote(down_out.at[j], down_in.at[j], d_send.at[j], d_recv.at[j], (ctx, grp - 2))

    for j in range(chunks):
        for d in range(1, plane):
            gather(j, d).start()
    moves = []
    if teacher_ref is not None:
        t_send, t_recv, t_own = more
        tokens = target_ref.shape[1]
        for d in range(1, groups):
            peer = (grp + d) % groups
            moves.append(remote(teacher_ref.at[pl.ds(peer * tokens, tokens)], target_ref.at[grp],
                                t_send.at[d - 1], t_recv.at[d - 1], (ctx, peer)))
        for move in moves:
            move.start()
        own = pltpu.make_async_copy(teacher_ref.at[pl.ds(grp * tokens, tokens)], target_ref.at[grp], t_own)
        own.start()
    for j in range(chunks):
        stage[j, mine] = in_ref[mine * chunks + j]

    def load(ref, j, k):
        scale, row2 = read_side(ref[j, k, rows:, :])
        return decode(ref[j, k, :rows, :], scale), row2

    def store(ref, j, k, state, row2):
        code, scale = encode(state)
        ref[j, k, :rows, :] = code
        ref[j, k, rows:, :] = side_rows(scale, row2)

    def chain(j, has_in, has_out, copy, in_buf, out_buf, kept, kept_row):
        @pl.when(has_in)
        def _():
            copy(j).wait_recv()
            for k in range(spans):
                state, row2 = load(in_buf, j, k)
                kept[j, k] = state
                kept_row[j, k] = row2

        @pl.when(jnp.logical_not(has_in))
        def _():
            for k in range(spans):
                kept[j, k] = jnp.zeros_like(kept[j, k])
                kept_row[j, k] = jnp.zeros_like(kept_row[j, k])

        @pl.when(has_out)
        def _():
            for k in range(spans):
                store(out_buf, j, k, kept[j, k] + total[j, k], kept_row[j, k] + total_row[j, k])
            copy(j).start()

    def step(t, unused):
        @pl.when(t < chunks)
        def _():
            for d in range(1, plane):
                gather(t, d).wait_recv()
            for k in range(spans):
                first, first_row = load(stage, t, 2 * k)
                second, second_row = load(stage, t, 2 * k + 1)
                total[t, k] = first + second
                total_row[t, k] = first_row + second_row

        j_up = t - level

        @pl.when((j_up >= 0) & (j_up < chunks))
        def _():
            chain(j_up, level > 0, level < depth - 1, upward, up_in, up_out, below, below_row)

        j_down = t - (depth - 1 - level)

        @pl.when((j_down >= 0) & (j_down < chunks))
        def _():
            chain(j_down, level < depth - 1, level > 0, downward, down_in, down_out, above, above_row)

        j_end = t - (depth - 1)

        @pl.when(j_end >= 0)
        def _():
            j = j_end
            run = jnp.zeros(total.shape[2:], F32)
            run_row = jnp.zeros(total_row.shape[2:], F32)
            for i in range(spans):
                k = spans - 1 - i if reverse else i
                near, near_row = (above, above_row) if reverse else (below, below_row)
                state, row2 = run + near[j, k], run_row + near_row[j, k]
                one, two = (2 * k + 1, 2 * k) if reverse else (2 * k, 2 * k + 1)
                store(back, j, one, state, row2)
                beside, beside_row = load(stage, j, one)
                store(back, j, two, state + beside, row2 + beside_row)
                run = run + below[j, k] + total[j, k] + above[j, k]
                run_row = run_row + below_row[j, k] + total_row[j, k] + above_row[j, k]
            for d in range(1, plane):
                scatter(j, d).start()
            out_ref[mine * chunks + j] = back[j, mine]

        return unused

    lax.fori_loop(0, chunks + depth - 1, step, 0)

    for j in range(chunks):
        for d in range(1, plane):
            gather(j, d).wait_send()
            scatter(j, d).wait()

    @pl.when(level < depth - 1)
    def _():
        for j in range(chunks):
            upward(j).wait_send()

    @pl.when(level > 0)
    def _():
        for j in range(chunks):
            downward(j).wait_send()

    if teacher_ref is not None:
        for move in moves:
            move.wait()
        own.wait()


def exchange(reverse, spans, depth, pieces, teacher=None):
    count, length, width = pieces.shape
    plane, groups = 2 * spans, 2 * depth
    chunks = count // plane
    vmem = pl.BlockSpec(memory_space=pltpu.VMEM)
    anywhere = pl.BlockSpec(memory_space=pl.ANY)
    in_specs, out_specs, args = [vmem], [vmem], [pieces]
    out_shape = [jax.ShapeDtypeStruct(pieces.shape, BF16)]
    dma = pltpu.SemaphoreType.DMA
    line = pltpu.VMEM((chunks, spans, length, width), BF16)
    wide = pltpu.VMEM((chunks, spans, length - SIDE, width), F32)
    row = pltpu.VMEM((chunks, spans, 2, width), F32)
    block = pltpu.VMEM((chunks, plane, length, width), BF16)
    scratch = [block, block, line, line, line, line, wide, wide, wide, row, row, row]
    scratch += [dma((chunks, plane - 1))] * 4 + [dma((chunks,))] * 4
    if teacher is not None:
        in_specs.append(anywhere)
        out_specs.append(anywhere)
        args.append(teacher)
        shape = (groups, teacher.shape[0] // groups, teacher.shape[1])
        out_shape.append(jax.ShapeDtypeStruct(shape, BF16))
        scratch += [dma((groups - 1,)), dma((groups - 1,)), dma]
    return pl.pallas_call(
        functools.partial(exchange_kernel, reverse, spans, depth),
        in_specs=in_specs,
        out_specs=out_specs,
        out_shape=out_shape,
        scratch_shapes=scratch,
        compiler_params=pltpu.CompilerParams(
            collective_id=1 if reverse else 0, has_side_effects=True, vmem_limit_bytes=56 * 1024 * 1024
        ),
        name="suffix_exchange" if reverse else "prefix_exchange",
    )(*args)


def forward_kernel(scale, q_ref, k_ref, v_ref, t_ref, before_ref, qg_ref, kl_ref, adj_ref):
    q, k, v = q_ref[...], k_ref[...], v_ref[...]
    kv, key_row = read_state(before_ref)
    kv_hi, kv_lo = split(kv)
    rows = q.shape[0]
    causal = lax.broadcasted_iota(jnp.int32, (rows, rows), 1) <= lax.broadcasted_iota(
        jnp.int32, (rows, rows), 0
    )
    q_wide = q.astype(F32)
    scores = jnp.where(causal, dot(q, k, NT), 0.0)
    s_hi, s_lo = split(scores)
    numer = dot(s_hi, v, NN) + dot(s_lo, v, NN) + dot(q, kv_hi, NN) + dot(q, kv_lo, NN)
    denom = jnp.sum(scores, axis=1, keepdims=True) + jnp.sum(q_wide * key_row, axis=1, keepdims=True)
    inv = 1.0 / denom
    student = numer * inv
    resid = student - t_ref[0].astype(F32)
    d_numer = resid * inv
    d_denom = -jnp.sum(resid * student, axis=1, keepdims=True) * inv
    dn_hi, dn_lo = split(d_numer)
    adj = dot(q, dn_hi, TN) + dot(q, dn_lo, TN)
    write_state(adj_ref, adj, jnp.sum(d_denom * q_wide, axis=0, keepdims=True))
    mixed = jnp.where(causal, dot(dn_hi, v, NT) + dot(dn_lo, v, NT) + d_denom, 0.0)
    m_hi, m_lo = split(mixed)
    q_grad = dot(m_hi, k, NN) + dot(m_lo, k, NN)
    q_grad = q_grad + dot(dn_hi, kv_hi, NT) + dot(dn_hi, kv_lo, NT) + dot(dn_lo, kv_hi, NT)
    q_grad = q_grad + d_denom * key_row
    qg_ref[...] = (scale * q_grad).astype(BF16)
    kl_ref[...] = dot(m_hi, q, TN) + dot(m_lo, q, TN)


def backward_kernel(scale, v_ref, kl_ref, after_ref, kg_ref):
    adj, row = read_state(after_ref)
    a_hi, a_lo = split(adj)
    v = v_ref[...]
    k_grad = kl_ref[...] + dot(v, a_hi, NT) + dot(v, a_lo, NT) + row
    kg_ref[...] = (scale * k_grad).astype(BF16)


def on_device(spans, groups, query_feat, key_feat, values, teacher):
    rows = query_feat.shape[0]
    feat = query_feat.shape[1] // H
    width = values.shape[1] // H
    scale = float(rows * spans * groups) ** 0.5
    depth = groups // 2
    per_head = feat // width
    per_group = H // groups
    params = pltpu.CompilerParams(vmem_limit_bytes=56 * 1024 * 1024)

    def cols(w):
        return pl.BlockSpec((rows, w), lambda h: (0, h))

    state_spec = pl.BlockSpec((per_head, width + SIDE, width), lambda h: (h, 0, 0))
    state_shape = jax.ShapeDtypeStruct((H * per_head, width + SIDE, width), BF16)
    target_spec = pl.BlockSpec((1, rows, width), lambda h: (h // per_group, 0, h % per_group))

    local = pl.pallas_call(
        local_kernel,
        grid=(H,),
        in_specs=[cols(feat), cols(width)],
        out_specs=state_spec,
        out_shape=state_shape,
        compiler_params=params,
        name="local_state",
    )(key_feat, values)
    before, target = exchange(False, spans, depth, local, teacher)
    query_grad, key_local, adj = pl.pallas_call(
        functools.partial(forward_kernel, scale),
        grid=(H,),
        in_specs=[cols(feat), cols(feat), cols(width), target_spec, state_spec],
        out_specs=[cols(feat), cols(feat), state_spec],
        out_shape=[
            jax.ShapeDtypeStruct((rows, H * feat), BF16),
            jax.ShapeDtypeStruct((rows, H * feat), F32),
            state_shape,
        ],
        compiler_params=params,
        name="forward",
    )(query_feat, key_feat, values, target, before)
    (after,) = exchange(True, spans, depth, adj)
    key_grad = pl.pallas_call(
        functools.partial(backward_kernel, scale),
        grid=(H,),
        in_specs=[cols(width), cols(feat), state_spec],
        out_specs=cols(feat),
        out_shape=jax.ShapeDtypeStruct((rows, H * feat), BF16),
        compiler_params=params,
        name="backward",
    )(values, key_local, after)
    return query_grad, key_grad


def solution(mesh):
    placed = (
        P(("ctx", "grp"), None),
        P(("ctx", "grp"), None),
        P(("ctx", "grp"), None),
        P("ctx", "grp"),
    )
    return jax.shard_map(
        functools.partial(on_device, mesh.shape["ctx"], mesh.shape["grp"]),
        mesh=mesh,
        in_specs=placed,
        out_specs=(P(("ctx", "grp"), None), P(("ctx", "grp"), None)),
        check_vma=False,
    )
```

```python
import functools

import jax
import jax.numpy as jnp
from jax import lax
from jax.experimental import pallas as pl
from jax.experimental.pallas import tpu as pltpu
from jax.sharding import PartitionSpec as P

H = 16
SIDE = 16
SPAN = 125.0
F32 = jnp.float32
BF16 = jnp.bfloat16


def dot(a, b, dims):
    return lax.dot_general(a, b, (dims, ((), ())), preferred_element_type=F32)


NN = ((1,), (0,))
NT = ((1,), (1,))
TN = ((0,), (0,))


def split(x):
    hi = x.astype(BF16)
    return hi, (x - hi.astype(F32)).astype(BF16)


def encode(x):
    scale = (jnp.maximum(jnp.max(jnp.abs(x), axis=0, keepdims=True), 1e-20) * 1.01).astype(BF16)
    y = jnp.exp2(jnp.abs(x) * (2 * SPAN / scale.astype(F32)) - SPAN)
    return jnp.where(x < 0, -y, y).astype(BF16), scale


def decode(code, scale):
    y = code.astype(F32)
    x = (jnp.log2(jnp.abs(y)) + SPAN) * (scale.astype(F32) * (0.5 / SPAN))
    return jnp.where(y < 0, -x, x)


def side_rows(scale, row2):
    hi = row2.astype(BF16).astype(F32)
    mid = (row2 - hi).astype(BF16).astype(F32)
    low = row2 - hi - mid
    pad = jnp.zeros((SIDE - 7, row2.shape[1]), F32)
    return jnp.concatenate([scale.astype(F32), hi, mid, low, pad], axis=0).astype(BF16)


def read_side(side):
    s = side.astype(F32)
    return s[0:1], s[1:3] + s[3:5] + s[5:7]


def write_state(ref, piece, state, row):
    width = state.shape[1]
    code, scale = encode(state)
    side = side_rows(scale, jnp.concatenate([row[:, :width], row[:, width:]], axis=0))
    for p in range(state.shape[0] // width):
        ref[piece + p, :width, :] = code[p * width : (p + 1) * width]
        ref[piece + p, width:, :] = side


def read_state(ref, piece, count):
    rows = ref.shape[1] - SIDE
    parts = []
    for p in range(count):
        scale, row2 = read_side(ref[piece + p, rows:, :])
        parts.append(decode(ref[piece + p, :rows, :], scale))
    return jnp.concatenate(parts, axis=0), jnp.concatenate([row2[0:1], row2[1:2]], axis=1)


def remote(src, dst, send, recv, to):
    return pltpu.make_async_remote_copy(
        src_ref=src, dst_ref=dst, send_sem=send, recv_sem=recv, device_id=to,
        device_id_type=pl.DeviceIdType.MESH,
    )


class Exchange:
    def __init__(self, reverse, spans, depth, buffers, kept):
        self.reverse, self.spans, self.depth = reverse, spans, depth
        (self.sent, self.got, self.stage, self.back, self.up_out, self.up_in, self.down_out,
         self.down_in, self.a_send, self.a_recv, self.b_send, self.b_recv, self.u_send,
         self.u_recv, self.d_send, self.d_recv) = buffers
        (self.total, self.above, self.below, self.total_row, self.above_row, self.below_row) = kept
        self.plane = 2 * spans
        self.chunks, self.rows = self.stage.shape[0], self.stage.shape[2] - SIDE
        self.steps = self.chunks + depth - 1
        self.ctx, self.grp = lax.axis_index("ctx"), lax.axis_index("grp")
        self.level = self.grp // 2
        self.mine = self.ctx * 2 + self.grp % 2

    def peer(self, d):
        return (self.mine + d) % self.plane

    def place(self, q):
        return (q // 2, self.level * 2 + q % 2)

    def gather(self, j, d):
        peer = self.peer(d)
        return remote(self.sent.at[peer * self.chunks + j], self.stage.at[j, self.mine],
                      self.a_send.at[j, d - 1], self.a_recv.at[j, d - 1], self.place(peer))

    def scatter(self, j, d):
        peer = self.peer(d)
        return remote(self.back.at[j, peer], self.got.at[self.mine * self.chunks + j],
                      self.b_send.at[j, d - 1], self.b_recv.at[j, d - 1], self.place(peer))

    def upward(self, j):
        return remote(self.up_out.at[j], self.up_in.at[j], self.u_send.at[j], self.u_recv.at[j],
                      (self.ctx, self.grp + 2))

    def downward(self, j):
        return remote(self.down_out.at[j], self.down_in.at[j], self.d_send.at[j],
                      self.d_recv.at[j], (self.ctx, self.grp - 2))

    def load(self, ref, j, k):
        scale, row2 = read_side(ref[j, k, self.rows :, :])
        return decode(ref[j, k, : self.rows, :], scale), row2

    def store(self, ref, j, k, state, row2):
        code, scale = encode(state)
        ref[j, k, : self.rows, :] = code
        ref[j, k, self.rows :, :] = side_rows(scale, row2)

    def chain(self, j, has_in, has_out, copy, in_buf, out_buf, kept, kept_row):
        @pl.when(has_in)
        def _():
            copy(j).wait_recv()
            for k in range(self.spans):
                kept[j, k], kept_row[j, k] = self.load(in_buf, j, k)

        @pl.when(jnp.logical_not(has_in))
        def _():
            for k in range(self.spans):
                kept[j, k] = jnp.zeros_like(kept[j, k])
                kept_row[j, k] = jnp.zeros_like(kept_row[j, k])

        @pl.when(has_out)
        def _():
            for k in range(self.spans):
                self.store(out_buf, j, k, kept[j, k] + self.total[j, k],
                           kept_row[j, k] + self.total_row[j, k])
            copy(j).start()

    def finish(self, j):
        near, near_row = (self.above, self.above_row) if self.reverse else (self.below, self.below_row)
        run = jnp.zeros(self.total.shape[2:], F32)
        run_row = jnp.zeros(self.total_row.shape[2:], F32)
        for i in range(self.spans):
            k = self.spans - 1 - i if self.reverse else i
            one, two = (2 * k + 1, 2 * k) if self.reverse else (2 * k, 2 * k + 1)
            state, row2 = run + near[j, k], run_row + near_row[j, k]
            self.store(self.back, j, one, state, row2)
            beside, beside_row = self.load(self.stage, j, one)
            self.store(self.back, j, two, state + beside, row2 + beside_row)
            run = run + self.below[j, k] + self.total[j, k] + self.above[j, k]
            run_row = run_row + self.below_row[j, k] + self.total_row[j, k] + self.above_row[j, k]
        for d in range(1, self.plane):
            self.scatter(j, d).start()
        self.got[self.mine * self.chunks + j] = self.back[j, self.mine]

    def run(self, beside):
        level, depth, chunks = self.level, self.depth, self.chunks

        def step(t, unused):
            @pl.when(t < chunks)
            def _():
                for d in range(1, self.plane):
                    self.gather(t, d).wait_recv()
                for k in range(self.spans):
                    first, first_row = self.load(self.stage, t, 2 * k)
                    second, second_row = self.load(self.stage, t, 2 * k + 1)
                    self.total[t, k] = first + second
                    self.total_row[t, k] = first_row + second_row

            j_up = t - level

            @pl.when((j_up >= 0) & (j_up < chunks))
            def _():
                self.chain(j_up, level > 0, level < depth - 1, self.upward, self.up_in,
                           self.up_out, self.below, self.below_row)

            j_down = t - (depth - 1 - level)

            @pl.when((j_down >= 0) & (j_down < chunks))
            def _():
                self.chain(j_down, level < depth - 1, level > 0, self.downward, self.down_in,
                           self.down_out, self.above, self.above_row)

            j_end = t - (depth - 1)

            @pl.when(j_end >= 0)
            def _():
                self.finish(j_end)

            beside(t + 1)
            return unused

        beside(0)
        lax.fori_loop(0, self.steps, step, 0)

    def each_head(self, work):
        per_head = 2
        for jj in range(self.chunks // per_head):

            def one(i, unused, jj=jj):
                peer = self.peer(i + 1)
                work(peer * (self.chunks // per_head) + jj, per_head * jj, i + 1)
                return unused

            lax.fori_loop(0, self.plane, one, 0)

    def send(self, chunk, d):
        @pl.when(d < self.plane)
        def _():
            self.gather(chunk, d).start()
            self.gather(chunk + 1, d).start()

        @pl.when(d == self.plane)
        def _():
            for j in (chunk, chunk + 1):
                self.stage[j, self.mine] = self.sent[self.mine * self.chunks + j]

    def receive(self, chunk, d):
        @pl.when(d < self.plane)
        def _():
            self.scatter(chunk, self.plane - d).wait_recv()
            self.scatter(chunk + 1, self.plane - d).wait_recv()

    def drain(self):
        for j in range(self.chunks):
            for d in range(1, self.plane):
                self.gather(j, d).wait_send()
                self.scatter(j, d).wait_send()

        @pl.when(self.level < self.depth - 1)
        def _():
            for j in range(self.chunks):
                self.upward(j).wait_send()

        @pl.when(self.level > 0)
        def _():
            for j in range(self.chunks):
                self.downward(j).wait_send()


def kernel(spans, depth, scale, q_ref, k_ref, v_ref, teacher_ref, qg_ref, kg_ref, *scratch):
    kept, first, second = scratch[:6], scratch[6:22], scratch[22:38]
    (target, numer_ref, denom_ref, hi_ref, lo_ref, dd_ref, kl_ref, t_send, t_recv, t_own) = scratch[38:]
    prefix = Exchange(False, spans, depth, first, kept)
    suffix = Exchange(True, spans, depth, second, kept)
    ctx, grp, plane, groups = prefix.ctx, prefix.grp, 2 * spans, 2 * depth
    rows = q_ref.shape[0]
    feat, width = q_ref.shape[1] // H, v_ref.shape[1] // H
    per_head = feat // width
    per_group = H // groups
    causal = lax.broadcasted_iota(jnp.int32, (rows, rows), 1) <= lax.broadcasted_iota(
        jnp.int32, (rows, rows), 0
    )

    def cols(head, w):
        return pl.ds(pl.multiple_of(head * w, w), w)

    def greet(to):
        pl.semaphore_signal(barrier, inc=1, device_id=to, device_id_type=pl.DeviceIdType.MESH)

    barrier = pltpu.get_barrier_semaphore()
    for d in range(1, plane):
        greet(prefix.place(prefix.peer(d)))
    for d in range(1, groups):
        greet((ctx, (grp + d) % groups))
    pl.semaphore_wait(barrier, plane + groups - 2)

    def give(d):
        peer = (grp + d) % groups
        return remote(teacher_ref.at[pl.ds(peer * rows, rows)], target.at[grp], t_send.at[d - 1],
                      t_recv.at[d - 1], (ctx, peer))

    own = pltpu.make_async_copy(teacher_ref.at[pl.ds(grp * rows, rows)], target.at[grp], t_own)
    own.start()

    def local(head, chunk, d):
        k = k_ref[:, cols(head, feat)]
        state = dot(k, v_ref[:, cols(head, width)], TN)
        write_state(prefix.sent, head * per_head, state, jnp.sum(k.astype(F32), axis=0, keepdims=True))
        prefix.send(chunk, d)

    prefix.each_head(local)

    def scores_of(head):
        q, k, v = q_ref[:, cols(head, feat)], k_ref[:, cols(head, feat)], v_ref[:, cols(head, width)]
        scores = jnp.where(causal, dot(q, k, NT), 0.0)
        s_hi, s_lo = split(scores)
        numer_ref[head] = dot(s_hi, v, NN) + dot(s_lo, v, NN)
        denom_ref[head] = jnp.sum(scores, axis=1, keepdims=True)

    def beside_prefix(t):
        for i in (1, 2):
            @pl.when(2 * t + i < groups)
            def _():
                give(2 * t + i).start()

        @pl.when(t < H // 2)
        def _():
            scores_of(2 * t)
            scores_of(2 * t + 1)

    prefix.run(beside_prefix)
    for t in range(prefix.steps + 1, max(H // 2, groups // 2)):
        beside_prefix(t)
    for d in range(1, groups):
        give(d).wait()
    own.wait()

    def forward(head, chunk, d):
        prefix.receive(chunk, d)
        q = q_ref[:, cols(head, feat)]
        q_wide = q.astype(F32)
        kv, key_row = read_state(prefix.got, head * per_head, per_head)
        kv_hi, kv_lo = split(kv)
        numer = numer_ref[head] + dot(q, kv_hi, NN) + dot(q, kv_lo, NN)
        denom = denom_ref[head] + jnp.sum(q_wide * key_row, axis=1, keepdims=True)
        inv = 1.0 / denom
        student = numer * inv
        resid = student - target[head // per_group, :, cols(head % per_group, width)].astype(F32)
        d_denom = -jnp.sum(resid * student, axis=1, keepdims=True) * inv
        dn_hi, dn_lo = split(resid * inv)
        hi_ref[head] = dn_hi
        lo_ref[head] = dn_lo
        dd_ref[head] = d_denom
        adj = dot(q, dn_hi, TN) + dot(q, dn_lo, TN)
        write_state(suffix.sent, head * per_head, adj, jnp.sum(d_denom * q_wide, axis=0, keepdims=True))
        suffix.send(chunk, d)

    prefix.each_head(forward)

    def grads_of(head):
        q, k, v = q_ref[:, cols(head, feat)], k_ref[:, cols(head, feat)], v_ref[:, cols(head, width)]
        dn_hi, dn_lo, d_denom = hi_ref[head], lo_ref[head], dd_ref[head]
        kv, key_row = read_state(prefix.got, head * per_head, per_head)
        kv_hi, kv_lo = split(kv)
        mixed = jnp.where(causal, dot(dn_hi, v, NT) + dot(dn_lo, v, NT) + d_denom, 0.0)
        m_hi, m_lo = split(mixed)
        q_grad = dot(m_hi, k, NN) + dot(m_lo, k, NN)
        q_grad = q_grad + dot(dn_hi, kv_hi, NT) + dot(dn_hi, kv_lo, NT) + dot(dn_lo, kv_hi, NT)
        q_grad = q_grad + d_denom * key_row
        qg_ref[:, cols(head, feat)] = (scale * q_grad).astype(BF16)
        kl_ref[head] = dot(m_hi, q, TN) + dot(m_lo, q, TN)

    def beside_suffix(t):
        @pl.when(t < H // 2)
        def _():
            grads_of(2 * t)
            grads_of(2 * t + 1)

    suffix.run(beside_suffix)
    for t in range(suffix.steps + 1, H // 2):
        beside_suffix(t)

    def backward(head, chunk, d):
        suffix.receive(chunk, d)
        adj, row = read_state(suffix.got, head * per_head, per_head)
        a_hi, a_lo = split(adj)
        v = v_ref[:, cols(head, width)]
        k_grad = kl_ref[head] + dot(v, a_hi, NT) + dot(v, a_lo, NT) + row
        kg_ref[:, cols(head, feat)] = (scale * k_grad).astype(BF16)

    suffix.each_head(backward)
    prefix.drain()
    suffix.drain()


def on_device(spans, groups, query_feat, key_feat, values, teacher):
    rows = query_feat.shape[0]
    feat = query_feat.shape[1] // H
    width = values.shape[1] // H
    scale = float(rows * spans * groups) ** 0.5
    depth, plane = groups // 2, 2 * spans
    pieces = H * feat // width
    chunks = pieces // plane
    length = width + SIDE
    dma = pltpu.SemaphoreType.DMA
    vmem = pl.BlockSpec(memory_space=pltpu.VMEM)
    whole = pltpu.VMEM((pieces, length, width), BF16)
    block = pltpu.VMEM((chunks, plane, length, width), BF16)
    line = pltpu.VMEM((chunks, spans, length, width), BF16)
    wide = pltpu.VMEM((chunks, spans, width, width), F32)
    row = pltpu.VMEM((chunks, spans, 2, width), F32)
    phase = [whole] * 2 + [block] * 2 + [line] * 4 + [dma((chunks, plane - 1))] * 4 + [dma((chunks,))] * 4
    column = pltpu.VMEM((H, rows, 1), F32)
    half = pltpu.VMEM((H, rows, width), BF16)
    scratch = [wide] * 3 + [row] * 3 + phase + phase + [
        pltpu.VMEM((groups, rows, teacher.shape[1]), BF16),
        pltpu.VMEM((H, rows, width), F32),
        column, half, half, column,
        pltpu.VMEM((H, rows, feat), F32),
        dma((groups - 1,)), dma((groups - 1,)), dma,
    ]
    out = jax.ShapeDtypeStruct((rows, H * feat), BF16)
    return pl.pallas_call(
        functools.partial(kernel, spans, depth, scale),
        in_specs=[vmem, vmem, vmem, pl.BlockSpec(memory_space=pl.ANY)],
        out_specs=[vmem, vmem],
        out_shape=[out, out],
        scratch_shapes=scratch,
        compiler_params=pltpu.CompilerParams(
            collective_id=0, has_side_effects=True, vmem_limit_bytes=60 * 1024 * 1024
        ),
        name="grads",
    )(query_feat, key_feat, values, teacher)


def solution(mesh):
    placed = (
        P(("ctx", "grp"), None),
        P(("ctx", "grp"), None),
        P(("ctx", "grp"), None),
        P("ctx", "grp"),
    )
    return jax.shard_map(
        functools.partial(on_device, mesh.shape["ctx"], mesh.shape["grp"]),
        mesh=mesh,
        in_specs=placed,
        out_specs=(P(("ctx", "grp"), None), P(("ctx", "grp"), None)),
        check_vma=False,
    )
```

```python
import functools

import jax
import jax.numpy as jnp
from jax import lax
from jax.experimental import pallas as pl
from jax.experimental.pallas import tpu as pltpu
from jax.sharding import PartitionSpec as P

H = 16
SIDE = 16
SPAN = 125.0
F32 = jnp.float32
BF16 = jnp.bfloat16


def dot(a, b, dims):
    return lax.dot_general(a, b, (dims, ((), ())), preferred_element_type=F32)


NN = ((1,), (0,))
NT = ((1,), (1,))
TN = ((0,), (0,))


def split(x):
    hi = x.astype(BF16)
    return hi, (x - hi.astype(F32)).astype(BF16)


def encode(x):
    scale = (jnp.maximum(jnp.max(jnp.abs(x), axis=0, keepdims=True), 1e-20) * 1.01).astype(BF16)
    y = jnp.exp2(jnp.abs(x) * (2 * SPAN / scale.astype(F32)) - SPAN)
    return jnp.where(x < 0, -y, y).astype(BF16), scale


def decode(code, scale):
    y = code.astype(F32)
    x = (jnp.log2(jnp.abs(y)) + SPAN) * (scale.astype(F32) * (0.5 / SPAN))
    return jnp.where(y < 0, -x, x)


def side_rows(scale, row2):
    hi = row2.astype(BF16).astype(F32)
    mid = (row2 - hi).astype(BF16).astype(F32)
    low = row2 - hi - mid
    pad = jnp.zeros((SIDE - 7, row2.shape[1]), F32)
    return jnp.concatenate([scale.astype(F32), hi, mid, low, pad], axis=0).astype(BF16)


def read_side(side):
    s = side.astype(F32)
    return s[0:1], s[1:3] + s[3:5] + s[5:7]


def write_state(ref, piece, state, row):
    width = state.shape[1]
    code, scale = encode(state)
    side = side_rows(scale, jnp.concatenate([row[:, :width], row[:, width:]], axis=0))
    for p in range(state.shape[0] // width):
        ref[piece + p, :width, :] = code[p * width : (p + 1) * width]
        ref[piece + p, width:, :] = side


def read_state(ref, piece, count):
    rows = ref.shape[1] - SIDE
    parts = []
    for p in range(count):
        scale, row2 = read_side(ref[piece + p, rows:, :])
        parts.append(decode(ref[piece + p, :rows, :], scale))
    return jnp.concatenate(parts, axis=0), jnp.concatenate([row2[0:1], row2[1:2]], axis=1)


def remote(src, dst, send, recv, to):
    return pltpu.make_async_remote_copy(
        src_ref=src, dst_ref=dst, send_sem=send, recv_sem=recv, device_id=to,
        device_id_type=pl.DeviceIdType.MESH,
    )


class Exchange:
    def __init__(self, reverse, spans, depth, buffers, kept):
        self.reverse, self.spans, self.depth = reverse, spans, depth
        (self.sent, self.got, self.stage, self.back, self.up_out, self.up_in, self.down_out,
         self.down_in, self.a_send, self.a_recv, self.b_send, self.b_recv, self.u_send,
         self.u_recv, self.d_send, self.d_recv) = buffers
        (self.total, self.above, self.below, self.total_row, self.above_row, self.below_row) = kept
        self.plane = 2 * spans
        self.chunks, self.rows = self.stage.shape[0], self.stage.shape[2] - SIDE
        self.steps = self.chunks + depth - 1
        self.ctx, self.grp = lax.axis_index("ctx"), lax.axis_index("grp")
        self.level = self.grp // 2
        self.mine = self.ctx * 2 + self.grp % 2

    def peer(self, d):
        return (self.mine + d) % self.plane

    def place(self, q):
        return (q // 2, self.level * 2 + q % 2)

    def gather(self, j, d):
        peer = self.peer(d)
        return remote(self.sent.at[peer * self.chunks + j], self.stage.at[j, self.mine],
                      self.a_send.at[j, d - 1], self.a_recv.at[j, d - 1], self.place(peer))

    def scatter(self, j, d):
        peer = self.peer(d)
        return remote(self.back.at[j, peer], self.got.at[self.mine * self.chunks + j],
                      self.b_send.at[j, d - 1], self.b_recv.at[j, d - 1], self.place(peer))

    def upward(self, j):
        return remote(self.up_out.at[j], self.up_in.at[j], self.u_send.at[j], self.u_recv.at[j],
                      (self.ctx, self.grp + 2))

    def downward(self, j):
        return remote(self.down_out.at[j], self.down_in.at[j], self.d_send.at[j],
                      self.d_recv.at[j], (self.ctx, self.grp - 2))

    def load(self, ref, j, k):
        scale, row2 = read_side(ref[j, k, self.rows :, :])
        return decode(ref[j, k, : self.rows, :], scale), row2

    def store(self, ref, j, k, state, row2):
        code, scale = encode(state)
        ref[j, k, : self.rows, :] = code
        ref[j, k, self.rows :, :] = side_rows(scale, row2)

    def chain(self, j, has_in, has_out, copy, in_buf, out_buf, kept, kept_row):
        @pl.when(has_in)
        def _():
            copy(j).wait_recv()
            for k in range(self.spans):
                kept[j, k], kept_row[j, k] = self.load(in_buf, j, k)

        @pl.when(jnp.logical_not(has_in))
        def _():
            for k in range(self.spans):
                kept[j, k] = jnp.zeros_like(kept[j, k])
                kept_row[j, k] = jnp.zeros_like(kept_row[j, k])

        @pl.when(has_out)
        def _():
            for k in range(self.spans):
                self.store(out_buf, j, k, kept[j, k] + self.total[j, k],
                           kept_row[j, k] + self.total_row[j, k])
            copy(j).start()

    def finish(self, j):
        near, near_row = (self.above, self.above_row) if self.reverse else (self.below, self.below_row)
        run = jnp.zeros(self.total.shape[2:], F32)
        run_row = jnp.zeros(self.total_row.shape[2:], F32)
        for i in range(self.spans):
            k = self.spans - 1 - i if self.reverse else i
            one, two = (2 * k + 1, 2 * k) if self.reverse else (2 * k, 2 * k + 1)
            state, row2 = run + near[j, k], run_row + near_row[j, k]
            self.store(self.back, j, one, state, row2)
            beside, beside_row = self.load(self.stage, j, one)
            self.store(self.back, j, two, state + beside, row2 + beside_row)
            run = run + self.below[j, k] + self.total[j, k] + self.above[j, k]
            run_row = run_row + self.below_row[j, k] + self.total_row[j, k] + self.above_row[j, k]
        for d in range(1, self.plane):
            self.scatter(j, d).start()
        self.got[self.mine * self.chunks + j] = self.back[j, self.mine]

    def step(self, t):
        level, depth, chunks = self.level, self.depth, self.chunks

        @pl.when((t >= 0) & (t < chunks))
        def _():
            for d in range(1, self.plane):
                self.gather(t, d).wait_recv()
            for k in range(self.spans):
                first, first_row = self.load(self.stage, t, 2 * k)
                second, second_row = self.load(self.stage, t, 2 * k + 1)
                self.total[t, k] = first + second
                self.total_row[t, k] = first_row + second_row

        j_up = t - level

        @pl.when((j_up >= 0) & (j_up < chunks))
        def _():
            self.chain(j_up, level > 0, level < depth - 1, self.upward, self.up_in,
                       self.up_out, self.below, self.below_row)

        j_down = t - (depth - 1 - level)

        @pl.when((j_down >= 0) & (j_down < chunks))
        def _():
            self.chain(j_down, level < depth - 1, level > 0, self.downward, self.down_in,
                       self.down_out, self.above, self.above_row)

        j_end = t - (depth - 1)

        @pl.when((j_end >= 0) & (j_end < chunks))
        def _():
            self.finish(j_end)

    def each_head(self, group, work):
        def one(i, unused):
            work(self.peer(i + 1) * (self.chunks // 2) + group, 2 * group, i + 1)
            return unused

        lax.fori_loop(0, self.plane, one, 0)

    def send(self, chunk, d):
        @pl.when(d < self.plane)
        def _():
            self.gather(chunk, d).start()
            self.gather(chunk + 1, d).start()

        @pl.when(d == self.plane)
        def _():
            for j in (chunk, chunk + 1):
                self.stage[j, self.mine] = self.sent[self.mine * self.chunks + j]

    def receive(self, chunk, d):
        @pl.when(d < self.plane)
        def _():
            self.scatter(chunk, self.plane - d).wait_recv()
            self.scatter(chunk + 1, self.plane - d).wait_recv()

    def drain(self):
        for j in range(self.chunks):
            for d in range(1, self.plane):
                self.gather(j, d).wait_send()
                self.scatter(j, d).wait_send()

        @pl.when(self.level < self.depth - 1)
        def _():
            for j in range(self.chunks):
                self.upward(j).wait_send()

        @pl.when(self.level > 0)
        def _():
            for j in range(self.chunks):
                self.downward(j).wait_send()


def kernel(spans, depth, scale, q_ref, k_ref, v_ref, teacher_ref, qg_ref, kg_ref, *scratch):
    first, second = scratch[:22], scratch[22:44]
    (target, numer_ref, denom_ref, hi_ref, lo_ref, dd_ref, kl_ref, t_send, t_recv, t_own) = scratch[44:]
    prefix = Exchange(False, spans, depth, first[6:], first[:6])
    suffix = Exchange(True, spans, depth, second[6:], second[:6])
    ctx, grp, plane, groups = prefix.ctx, prefix.grp, 2 * spans, 2 * depth
    rows = q_ref.shape[0]
    feat, width = q_ref.shape[1] // H, v_ref.shape[1] // H
    per_head = feat // width
    per_group = H // groups
    heads_each = H // plane
    causal = lax.broadcasted_iota(jnp.int32, (rows, rows), 1) <= lax.broadcasted_iota(
        jnp.int32, (rows, rows), 0
    )

    def cols(head, w):
        return pl.ds(pl.multiple_of(head * w, w), w)

    def greet(to):
        pl.semaphore_signal(barrier, inc=1, device_id=to, device_id_type=pl.DeviceIdType.MESH)

    barrier = pltpu.get_barrier_semaphore()
    for d in range(1, plane):
        greet(prefix.place(prefix.peer(d)))
    for d in range(1, groups):
        greet((ctx, (grp + d) % groups))
    pl.semaphore_wait(barrier, plane + groups - 2)

    def give(d):
        peer = (grp + d) % groups
        return remote(teacher_ref.at[pl.ds(peer * rows, rows)], target.at[grp], t_send.at[d - 1],
                      t_recv.at[d - 1], (ctx, peer))

    own = pltpu.make_async_copy(teacher_ref.at[pl.ds(grp * rows, rows)], target.at[grp], t_own)
    own.start()
    for d in range(2, groups, 2):
        give(d).start()

    def local(head, chunk, d):
        k = k_ref[:, cols(head, feat)]
        state = dot(k, v_ref[:, cols(head, width)], TN)
        write_state(prefix.sent, head * per_head, state, jnp.sum(k.astype(F32), axis=0, keepdims=True))
        prefix.send(chunk, d)

    for group in range(heads_each):
        prefix.each_head(group, local)

    def scores_of(head):
        q, k, v = q_ref[:, cols(head, feat)], k_ref[:, cols(head, feat)], v_ref[:, cols(head, width)]
        scores = jnp.where(causal, dot(q, k, NT), 0.0)
        s_hi, s_lo = split(scores)
        numer_ref[head] = dot(s_hi, v, NN) + dot(s_lo, v, NN)
        denom_ref[head] = jnp.sum(scores, axis=1, keepdims=True)

    def forward(head, chunk, d):
        prefix.receive(chunk, d)
        q = q_ref[:, cols(head, feat)]
        q_wide = q.astype(F32)
        kv, key_row = read_state(prefix.got, head * per_head, per_head)
        kv_hi, kv_lo = split(kv)
        numer = numer_ref[head] + dot(q, kv_hi, NN) + dot(q, kv_lo, NN)
        denom = denom_ref[head] + jnp.sum(q_wide * key_row, axis=1, keepdims=True)
        inv = 1.0 / denom
        student = numer * inv
        resid = student - target[head // per_group, :, cols(head % per_group, width)].astype(F32)
        d_denom = -jnp.sum(resid * student, axis=1, keepdims=True) * inv
        dn_hi, dn_lo = split(resid * inv)
        hi_ref[head] = dn_hi
        lo_ref[head] = dn_lo
        dd_ref[head] = d_denom
        adj = dot(q, dn_hi, TN) + dot(q, dn_lo, TN)
        write_state(suffix.sent, head * per_head, adj, jnp.sum(d_denom * q_wide, axis=0, keepdims=True))
        suffix.send(chunk, d)

    def grads_of(head):
        q, k, v = q_ref[:, cols(head, feat)], k_ref[:, cols(head, feat)], v_ref[:, cols(head, width)]
        dn_hi, dn_lo, d_denom = hi_ref[head], lo_ref[head], dd_ref[head]
        kv, key_row = read_state(prefix.got, head * per_head, per_head)
        kv_hi, kv_lo = split(kv)
        mixed = jnp.where(causal, dot(dn_hi, v, NT) + dot(dn_lo, v, NT) + d_denom, 0.0)
        m_hi, m_lo = split(mixed)
        q_grad = dot(m_hi, k, NN) + dot(m_lo, k, NN)
        q_grad = q_grad + dot(dn_hi, kv_hi, NT) + dot(dn_hi, kv_lo, NT) + dot(dn_lo, kv_hi, NT)
        q_grad = q_grad + d_denom * key_row
        qg_ref[:, cols(head, feat)] = (scale * q_grad).astype(BF16)
        kl_ref[head] = dot(m_hi, q, TN) + dot(m_lo, q, TN)

    def grads_at(i):
        grads_of(i % plane * heads_each + i // plane)

    steps, begin = prefix.steps, depth + 2
    quick, slow = 4, min(2, H // steps)

    def scores_at(t):
        @pl.when(t < H // quick)
        def _():
            for i in range(quick):
                scores_of(quick * t + i)

    def step(t, unused):
        prefix.step(t)

        @pl.when(2 * t + 1 < groups)
        def _():
            give(2 * t + 1).start()

        scores_at(t + 1)
        for group in range(heads_each):

            @pl.when(t == depth + 1 + 2 * group)
            def _():
                if group == 0:
                    for d in range(1, groups):
                        give(d).wait()
                    own.wait()
                prefix.each_head(group, forward)

        suffix.step(t - begin)

        @pl.when(t >= begin)
        def _():
            for i in range(slow):
                grads_at(slow * (t - begin) + i)

        return unused

    scores_at(0)
    lax.fori_loop(0, begin + steps, step, 0)
    for i in range(slow * steps, H):
        grads_at(i)

    def backward(head, chunk, d):
        suffix.receive(chunk, d)
        adj, row = read_state(suffix.got, head * per_head, per_head)
        a_hi, a_lo = split(adj)
        v = v_ref[:, cols(head, width)]
        k_grad = kl_ref[head] + dot(v, a_hi, NT) + dot(v, a_lo, NT) + row
        kg_ref[:, cols(head, feat)] = (scale * k_grad).astype(BF16)

    for group in range(heads_each):
        suffix.each_head(group, backward)
    prefix.drain()
    suffix.drain()


def on_device(spans, groups, query_feat, key_feat, values, teacher):
    rows = query_feat.shape[0]
    feat = query_feat.shape[1] // H
    width = values.shape[1] // H
    scale = float(rows * spans * groups) ** 0.5
    depth, plane = groups // 2, 2 * spans
    pieces = H * feat // width
    chunks = pieces // plane
    length = width + SIDE
    dma = pltpu.SemaphoreType.DMA
    vmem = pl.BlockSpec(memory_space=pltpu.VMEM)
    whole = pltpu.VMEM((pieces, length, width), BF16)
    block = pltpu.VMEM((chunks, plane, length, width), BF16)
    line = pltpu.VMEM((chunks, spans, length, width), BF16)
    wide = pltpu.VMEM((chunks, spans, width, width), F32)
    row = pltpu.VMEM((chunks, spans, 2, width), F32)
    phase = [wide] * 3 + [row] * 3 + [whole] * 2 + [block] * 2 + [line] * 4 + [dma((chunks, plane - 1))] * 4 + [dma((chunks,))] * 4
    column = pltpu.VMEM((H, rows, 1), F32)
    half = pltpu.VMEM((H, rows, width), BF16)
    scratch = phase + phase + [
        pltpu.VMEM((groups, rows, teacher.shape[1]), BF16),
        pltpu.VMEM((H, rows, width), F32),
        column, half, half, column,
        pltpu.VMEM((H, rows, feat), F32),
        dma((groups - 1,)), dma((groups - 1,)), dma,
    ]
    out = jax.ShapeDtypeStruct((rows, H * feat), BF16)
    return pl.pallas_call(
        functools.partial(kernel, spans, depth, scale),
        in_specs=[vmem, vmem, vmem, pl.BlockSpec(memory_space=pl.ANY)],
        out_specs=[vmem, vmem],
        out_shape=[out, out],
        scratch_shapes=scratch,
        compiler_params=pltpu.CompilerParams(
            collective_id=0, has_side_effects=True, vmem_limit_bytes=60 * 1024 * 1024
        ),
        name="grads",
    )(query_feat, key_feat, values, teacher)


def solution(mesh):
    placed = (
        P(("ctx", "grp"), None),
        P(("ctx", "grp"), None),
        P(("ctx", "grp"), None),
        P("ctx", "grp"),
    )
    return jax.shard_map(
        functools.partial(on_device, mesh.shape["ctx"], mesh.shape["grp"]),
        mesh=mesh,
        in_specs=placed,
        out_specs=(P(("ctx", "grp"), None), P(("ctx", "grp"), None)),
        check_vma=False,
    )
```

```python
import functools

import jax
import jax.numpy as jnp
from jax import lax
from jax.experimental import pallas as pl
from jax.experimental.pallas import tpu as pltpu
from jax.sharding import PartitionSpec as P

H = 16
SIDE = 16
SPAN = 125.0
F32 = jnp.float32
BF16 = jnp.bfloat16


def dot(a, b, dims):
    return lax.dot_general(a, b, (dims, ((), ())), preferred_element_type=F32)


NN = ((1,), (0,))
NT = ((1,), (1,))
TN = ((0,), (0,))


def split(x):
    hi = x.astype(BF16)
    return hi, (x - hi.astype(F32)).astype(BF16)


def encode(x):
    scale = (jnp.maximum(jnp.max(jnp.abs(x), axis=0, keepdims=True), 1e-20) * 1.01).astype(BF16)
    y = jnp.exp2(jnp.abs(x) * (2 * SPAN / scale.astype(F32)) - SPAN)
    return jnp.where(x < 0, -y, y).astype(BF16), scale


def decode(code, scale):
    y = code.astype(F32)
    x = (jnp.log2(jnp.abs(y)) + SPAN) * (scale.astype(F32) * (0.5 / SPAN))
    return jnp.where(y < 0, -x, x)


def side_rows(scale, row2):
    hi = row2.astype(BF16).astype(F32)
    mid = (row2 - hi).astype(BF16).astype(F32)
    low = row2 - hi - mid
    pad = jnp.zeros((SIDE - 7, row2.shape[1]), F32)
    return jnp.concatenate([scale.astype(F32), hi, mid, low, pad], axis=0).astype(BF16)


def read_side(side):
    s = side.astype(F32)
    return s[0:1], s[1:3] + s[3:5] + s[5:7]


def write_state(ref, piece, state, row):
    width = state.shape[1]
    code, scale = encode(state)
    side = side_rows(scale, jnp.concatenate([row[:, :width], row[:, width:]], axis=0))
    for p in range(state.shape[0] // width):
        ref[piece + p, :width, :] = code[p * width : (p + 1) * width]
        ref[piece + p, width:, :] = side


def read_state(ref, piece, count):
    rows = ref.shape[1] - SIDE
    parts = []
    for p in range(count):
        scale, row2 = read_side(ref[piece + p, rows:, :])
        parts.append(decode(ref[piece + p, :rows, :], scale))
    return jnp.concatenate(parts, axis=0), jnp.concatenate([row2[0:1], row2[1:2]], axis=1)


def remote(src, dst, send, recv, to):
    return pltpu.make_async_remote_copy(
        src_ref=src, dst_ref=dst, send_sem=send, recv_sem=recv, device_id=to,
        device_id_type=pl.DeviceIdType.MESH,
    )


class Exchange:
    def __init__(self, reverse, spans, depth, buffers, kept):
        self.reverse, self.spans, self.depth = reverse, spans, depth
        (self.sent, self.got, self.stage, self.back, self.up_out, self.up_in, self.down_out,
         self.down_in, self.a_send, self.a_recv, self.b_send, self.b_recv, self.u_send,
         self.u_recv, self.d_send, self.d_recv) = buffers
        (self.total, self.above, self.below, self.total_row, self.above_row, self.below_row) = kept
        self.plane = 2 * spans
        self.chunks, self.rows = self.back.shape[0], self.back.shape[2] - SIDE
        self.steps = self.chunks + depth - 1
        self.ctx, self.grp = lax.axis_index("ctx"), lax.axis_index("grp")
        self.level = lax.div(self.grp, 2)
        self.mine = self.ctx * 2 + lax.rem(self.grp, 2)
        self.peers = [self.peer(d) for d in range(self.plane)]
        self.places = [self.place(q) for q in self.peers]

    def peer(self, d):
        return lax.rem(self.mine + d, self.plane)

    def place(self, q):
        return (lax.div(q, 2), self.level * 2 + lax.rem(q, 2))

    def at(self, d):
        if isinstance(d, int):
            return self.peers[d], self.places[d]
        return self.peer(d), self.place(self.peer(d))

    def gather(self, g, d):
        peer, place = self.at(d)
        return remote(self.sent.at[pl.ds(peer * self.chunks + 2 * g, 2)], self.stage.at[g, self.mine],
                      self.a_send.at[g, d - 1], self.a_recv.at[g, d - 1], place)

    def scatter(self, j, d):
        peer, place = self.at(d)
        return remote(self.back.at[j, peer], self.got.at[self.mine * self.chunks + j],
                      self.b_send.at[j, d - 1], self.b_recv.at[j, d - 1], place)

    def upward(self, j):
        return remote(self.up_out.at[j], self.up_in.at[j], self.u_send.at[j], self.u_recv.at[j],
                      (self.ctx, self.grp + 2))

    def downward(self, j):
        return remote(self.down_out.at[j], self.down_in.at[j], self.d_send.at[j],
                      self.d_recv.at[j], (self.ctx, self.grp - 2))

    def load(self, ref, j, k):
        scale, row2 = read_side(ref[j, k, self.rows :, :])
        return decode(ref[j, k, : self.rows, :], scale), row2

    def staged(self, j, k):
        half, side = lax.div(j, 2), lax.rem(j, 2)
        scale, row2 = read_side(self.stage[half, k, side, self.rows :, :])
        return decode(self.stage[half, k, side, : self.rows, :], scale), row2

    def store(self, ref, j, k, state, row2):
        code, scale = encode(state)
        ref[j, k, : self.rows, :] = code
        ref[j, k, self.rows :, :] = side_rows(scale, row2)

    def chain(self, j, has_in, has_out, copy, in_buf, out_buf, kept, kept_row):
        @pl.when(has_in)
        def _():
            copy(j).wait_recv()
            for k in range(self.spans):
                kept[j, k], kept_row[j, k] = self.load(in_buf, j, k)

        @pl.when(jnp.logical_not(has_in))
        def _():
            for k in range(self.spans):
                kept[j, k] = jnp.zeros_like(kept[j, k])
                kept_row[j, k] = jnp.zeros_like(kept_row[j, k])

        @pl.when(has_out)
        def _():
            for k in range(self.spans):
                self.store(out_buf, j, k, kept[j, k] + self.total[j, k],
                           kept_row[j, k] + self.total_row[j, k])
            copy(j).start()

    def finish(self, j):
        near, near_row = (self.above, self.above_row) if self.reverse else (self.below, self.below_row)
        run = jnp.zeros(self.total.shape[2:], F32)
        run_row = jnp.zeros(self.total_row.shape[2:], F32)
        for i in range(self.spans):
            k = self.spans - 1 - i if self.reverse else i
            one, two = (2 * k + 1, 2 * k) if self.reverse else (2 * k, 2 * k + 1)
            state, row2 = run + near[j, k], run_row + near_row[j, k]
            self.store(self.back, j, one, state, row2)
            beside, beside_row = self.staged(j, one)
            self.store(self.back, j, two, state + beside, row2 + beside_row)
            run = run + self.below[j, k] + self.total[j, k] + self.above[j, k]
            run_row = run_row + self.below_row[j, k] + self.total_row[j, k] + self.above_row[j, k]
        for d in range(1, self.plane):
            self.scatter(j, d).start()
        self.got[self.mine * self.chunks + j] = self.back[j, self.mine]

    def step(self, t):
        level, depth, chunks = self.level, self.depth, self.chunks

        @pl.when((t >= 0) & (t < chunks) & (lax.rem(t, 2) == 0))
        def _():
            for d in range(1, self.plane):
                self.gather(lax.div(t, 2), d).wait_recv()

        @pl.when((t >= 0) & (t < chunks))
        def _():
            for k in range(self.spans):
                first, first_row = self.staged(t, 2 * k)
                second, second_row = self.staged(t, 2 * k + 1)
                self.total[t, k] = first + second
                self.total_row[t, k] = first_row + second_row

        j_up = t - level

        @pl.when((j_up >= 0) & (j_up < chunks))
        def _():
            self.chain(j_up, level > 0, level < depth - 1, self.upward, self.up_in,
                       self.up_out, self.below, self.below_row)

        j_down = t - (depth - 1 - level)

        @pl.when((j_down >= 0) & (j_down < chunks))
        def _():
            self.chain(j_down, level < depth - 1, level > 0, self.downward, self.down_in,
                       self.down_out, self.above, self.above_row)

        j_end = t - (depth - 1)

        @pl.when((j_end >= 0) & (j_end < chunks))
        def _():
            self.finish(j_end)

    def each_head(self, group, work):
        def one(i, unused):
            work(self.peer(i + 1) * (self.chunks // 2) + group, 2 * group, i + 1)
            return unused

        lax.fori_loop(0, self.plane, one, 0)

    def send(self, chunk, d):
        @pl.when(d < self.plane)
        def _():
            self.gather(chunk // 2, d).start()

        @pl.when(d == self.plane)
        def _():
            for i in range(2):
                self.stage[chunk // 2, self.mine, i] = self.sent[self.mine * self.chunks + chunk + i]

    def receive(self, chunk, d):
        @pl.when(d < self.plane)
        def _():
            self.scatter(chunk, self.plane - d).wait_recv()
            self.scatter(chunk + 1, self.plane - d).wait_recv()

    def drain(self):
        for j in range(self.chunks):
            for d in range(1, self.plane):
                self.scatter(j, d).wait_send()
        for g in range(self.chunks // 2):
            for d in range(1, self.plane):
                self.gather(g, d).wait_send()

        @pl.when(self.level < self.depth - 1)
        def _():
            for j in range(self.chunks):
                self.upward(j).wait_send()

        @pl.when(self.level > 0)
        def _():
            for j in range(self.chunks):
                self.downward(j).wait_send()


def kernel(spans, depth, scale, q_hbm, k_hbm, v_hbm, teacher_ref, qg_ref, kg_ref, q_ref, k_ref, v_ref, in_sem, *scratch):
    loads = [
        pltpu.make_async_copy(src, dst, in_sem.at[i])
        for i, (src, dst) in enumerate(((k_hbm, k_ref), (v_hbm, v_ref), (q_hbm, q_ref)))
    ]
    for load in loads:
        load.start()
    first, second = scratch[:22], scratch[22:44]
    (target, numer_ref, denom_ref, hi_ref, lo_ref, dd_ref, kl_ref, t_send, t_recv, t_own) = scratch[44:]
    prefix = Exchange(False, spans, depth, first[6:], first[:6])
    suffix = Exchange(True, spans, depth, second[6:], second[:6])
    ctx, grp, plane, groups = prefix.ctx, prefix.grp, 2 * spans, 2 * depth
    rows = q_ref.shape[0]
    feat, width = q_ref.shape[1] // H, v_ref.shape[1] // H
    per_head = feat // width
    per_group = H // groups
    heads_each = H // plane
    causal = lax.broadcasted_iota(jnp.int32, (rows, rows), 1) <= lax.broadcasted_iota(
        jnp.int32, (rows, rows), 0
    )

    def cols(head, w):
        return pl.ds(pl.multiple_of(head * w, w), w)

    def greet(to):
        pl.semaphore_signal(barrier, inc=1, device_id=to, device_id_type=pl.DeviceIdType.MESH)

    barrier = pltpu.get_barrier_semaphore()
    for d in range(1, plane):
        greet(prefix.places[d])
    for d in range(1, groups):
        greet((ctx, lax.rem(grp + d, groups)))
    pl.semaphore_wait(barrier, plane + groups - 2)

    def give(d):
        peer = lax.rem(grp + d, groups)
        return remote(teacher_ref.at[pl.ds(peer * rows, rows)], target.at[grp], t_send.at[d - 1],
                      t_recv.at[d - 1], (ctx, peer))

    own = pltpu.make_async_copy(teacher_ref.at[pl.ds(grp * rows, rows)], target.at[grp], t_own)
    own.start()
    for d in range(2, groups, 2):
        give(d).start()

    loads[0].wait()
    loads[1].wait()

    def local(head, chunk, d):
        k = k_ref[:, cols(head, feat)]
        state = dot(k, v_ref[:, cols(head, width)], TN)
        write_state(prefix.sent, head * per_head, state, jnp.sum(k.astype(F32), axis=0, keepdims=True))
        prefix.send(chunk, d)

    for group in range(heads_each):
        prefix.each_head(group, local)

    def scores_of(head):
        q, k, v = q_ref[:, cols(head, feat)], k_ref[:, cols(head, feat)], v_ref[:, cols(head, width)]
        scores = jnp.where(causal, dot(q, k, NT), 0.0)
        s_hi, s_lo = split(scores)
        numer_ref[head] = dot(s_hi, v, NN) + dot(s_lo, v, NN)
        denom_ref[head] = jnp.sum(scores, axis=1, keepdims=True)

    def forward(head, chunk, d):
        prefix.receive(chunk, d)
        q = q_ref[:, cols(head, feat)]
        q_wide = q.astype(F32)
        kv, key_row = read_state(prefix.got, head * per_head, per_head)
        kv_hi, kv_lo = split(kv)
        numer = numer_ref[head] + dot(q, kv_hi, NN) + dot(q, kv_lo, NN)
        denom = denom_ref[head] + jnp.sum(q_wide * key_row, axis=1, keepdims=True)
        inv = 1.0 / denom
        student = numer * inv
        resid = student - target[lax.div(head, per_group), :, cols(lax.rem(head, per_group), width)].astype(F32)
        d_denom = -jnp.sum(resid * student, axis=1, keepdims=True) * inv
        dn_hi, dn_lo = split(resid * inv)
        hi_ref[head] = dn_hi
        lo_ref[head] = dn_lo
        dd_ref[head] = d_denom
        adj = dot(q, dn_hi, TN) + dot(q, dn_lo, TN)
        write_state(suffix.sent, head * per_head, adj, jnp.sum(d_denom * q_wide, axis=0, keepdims=True))
        suffix.send(chunk, d)

    def grads_of(head):
        q, k, v = q_ref[:, cols(head, feat)], k_ref[:, cols(head, feat)], v_ref[:, cols(head, width)]
        dn_hi, dn_lo, d_denom = hi_ref[head], lo_ref[head], dd_ref[head]
        kv, key_row = read_state(prefix.got, head * per_head, per_head)
        kv_hi, kv_lo = split(kv)
        mixed = jnp.where(causal, dot(dn_hi, v, NT) + dot(dn_lo, v, NT) + d_denom, 0.0)
        m_hi, m_lo = split(mixed)
        q_grad = dot(m_hi, k, NN) + dot(m_lo, k, NN)
        q_grad = q_grad + dot(dn_hi, kv_hi, NT) + dot(dn_hi, kv_lo, NT) + dot(dn_lo, kv_hi, NT)
        q_grad = q_grad + d_denom * key_row
        qg_ref[:, cols(head, feat)] = (scale * q_grad).astype(BF16)
        kl_ref[head] = dot(m_hi, q, TN) + dot(m_lo, q, TN)

    def grads_at(i):
        grads_of(lax.rem(i, plane) * heads_each + lax.div(i, plane))

    steps, begin = prefix.steps, depth + 2
    quick, slow = 4, min(2, H // steps)

    def scores_at(t):
        @pl.when(t < H // quick)
        def _():
            for i in range(quick):
                scores_of(quick * t + i)

    def step(t, unused):
        prefix.step(t)

        @pl.when(2 * t + 1 < groups)
        def _():
            give(2 * t + 1).start()

        scores_at(t + 1)
        for group in range(heads_each):

            @pl.when(t == depth + 1 + 2 * group)
            def _():
                if group == 0:
                    for d in range(1, groups):
                        give(d).wait()
                    own.wait()
                prefix.each_head(group, forward)

        suffix.step(t - begin)

        @pl.when(t >= begin)
        def _():
            for i in range(slow):
                grads_at(slow * (t - begin) + i)

        return unused

    loads[2].wait()
    scores_at(0)
    lax.fori_loop(0, begin + steps, step, 0)
    for i in range(slow * steps, H):
        grads_of(i % plane * heads_each + i // plane)

    def backward(head, chunk, d):
        suffix.receive(chunk, d)
        adj, row = read_state(suffix.got, head * per_head, per_head)
        a_hi, a_lo = split(adj)
        v = v_ref[:, cols(head, width)]
        k_grad = kl_ref[head] + dot(v, a_hi, NT) + dot(v, a_lo, NT) + row
        kg_ref[:, cols(head, feat)] = (scale * k_grad).astype(BF16)

    for group in range(heads_each):
        suffix.each_head(group, backward)
    prefix.drain()
    suffix.drain()


def deliver_kernel(q_in, k_in, q_out, k_out):
    q_out[...] = q_in[...]
    k_out[...] = k_in[...]


def on_device(spans, groups, query_feat, key_feat, values, teacher):
    rows = query_feat.shape[0]
    feat = query_feat.shape[1] // H
    width = values.shape[1] // H
    scale = float(rows * spans * groups) ** 0.5
    depth, plane = groups // 2, 2 * spans
    pieces = H * feat // width
    chunks = pieces // plane
    length = width + SIDE
    dma = pltpu.SemaphoreType.DMA
    vmem = pl.BlockSpec(memory_space=pltpu.VMEM)
    whole = pltpu.VMEM((pieces, length, width), BF16)
    block = pltpu.VMEM((chunks, plane, length, width), BF16)
    line = pltpu.VMEM((chunks, spans, length, width), BF16)
    wide = pltpu.VMEM((chunks, spans, width, width), F32)
    row = pltpu.VMEM((chunks, spans, 2, width), F32)
    pairs = pltpu.VMEM((chunks // 2, plane, 2, length, width), BF16)
    phase = [wide] * 3 + [row] * 3 + [whole] * 2 + [pairs, block] + [line] * 4
    phase += [dma((chunks // 2, plane - 1))] * 2 + [dma((chunks, plane - 1))] * 2 + [dma((chunks,))] * 4
    column = pltpu.VMEM((H, rows, 1), F32)
    half = pltpu.VMEM((H, rows, width), BF16)
    scratch = [pltpu.VMEM(x.shape, BF16) for x in (query_feat, key_feat, values)] + [dma((3,))]
    scratch += phase + phase + [
        pltpu.VMEM((groups, rows, teacher.shape[1]), BF16),
        pltpu.VMEM((H, rows, width), F32),
        column, half, half, column,
        pltpu.VMEM((H, rows, feat), F32),
        dma((groups - 1,)), dma((groups - 1,)), dma,
    ]
    out = jax.ShapeDtypeStruct((rows, H * feat), BF16)
    grads = pl.pallas_call(
        functools.partial(kernel, spans, depth, scale),
        in_specs=[pl.BlockSpec(memory_space=pl.ANY)] * 4,
        out_specs=[vmem, vmem],
        out_shape=[out, out],
        scratch_shapes=scratch,
        compiler_params=pltpu.CompilerParams(
            collective_id=0, has_side_effects=True, vmem_limit_bytes=60 * 1024 * 1024
        ),
        name="grads",
    )(query_feat, key_feat, values, teacher)
    slab = pl.BlockSpec((rows // 4, H * feat), lambda i: (i, 0))
    return pl.pallas_call(
        deliver_kernel,
        grid=(4,),
        in_specs=[slab, slab],
        out_specs=[slab, slab],
        out_shape=[out, out],
        compiler_params=pltpu.CompilerParams(vmem_limit_bytes=60 * 1024 * 1024),
        name="deliver",
    )(*grads)


def solution(mesh):
    placed = (
        P(("ctx", "grp"), None),
        P(("ctx", "grp"), None),
        P(("ctx", "grp"), None),
        P("ctx", "grp"),
    )
    return jax.shard_map(
        functools.partial(on_device, mesh.shape["ctx"], mesh.shape["grp"]),
        mesh=mesh,
        in_specs=placed,
        out_specs=(P(("ctx", "grp"), None), P(("ctx", "grp"), None)),
        check_vma=False,
    )
```

```python
import functools

import jax
import jax.numpy as jnp
from jax import lax
from jax.experimental import pallas as pl
from jax.experimental.pallas import tpu as pltpu
from jax.sharding import PartitionSpec as P

H = 16
SIDE = 16
SPAN = 125.0
F32 = jnp.float32
BF16 = jnp.bfloat16


def dot(a, b, dims):
    return lax.dot_general(a, b, (dims, ((), ())), preferred_element_type=F32)


NN = ((1,), (0,))
NT = ((1,), (1,))
TN = ((0,), (0,))


def split(x):
    hi = x.astype(BF16)
    return hi, (x - hi.astype(F32)).astype(BF16)


def beside(a, b):
    return jnp.concatenate([a, b], axis=1)


def fold(x):
    half = x.shape[1] // 2
    return x[:, :half] + x[:, half:]


def encode(x):
    scale = (jnp.maximum(jnp.max(jnp.abs(x), axis=0, keepdims=True), 1e-20) * 1.01).astype(BF16)
    y = jnp.exp2(jnp.abs(x) * (2 * SPAN / scale.astype(F32)) - SPAN)
    return jnp.where(x < 0, -y, y).astype(BF16), scale


def decode(code, scale):
    y = code.astype(F32)
    x = (jnp.log2(jnp.abs(y)) + SPAN) * (scale.astype(F32) * (0.5 / SPAN))
    return jnp.where(y < 0, -x, x)


def side_rows(scale, row2):
    hi = row2.astype(BF16).astype(F32)
    mid = (row2 - hi).astype(BF16).astype(F32)
    low = row2 - hi - mid
    pad = jnp.zeros((SIDE - 7, row2.shape[1]), F32)
    return jnp.concatenate([scale.astype(F32), hi, mid, low, pad], axis=0).astype(BF16)


def read_side(side):
    s = side.astype(F32)
    return s[0:1], s[1:3] + s[3:5] + s[5:7]


def write_state(ref, piece, state, row):
    width = state.shape[1]
    code, scale = encode(state)
    side = side_rows(scale, jnp.concatenate([row[:, :width], row[:, width:]], axis=0))
    for p in range(state.shape[0] // width):
        ref[piece + p, :width, :] = code[p * width : (p + 1) * width]
        ref[piece + p, width:, :] = side


def read_state(ref, piece, count):
    rows = ref.shape[1] - SIDE
    parts = []
    for p in range(count):
        scale, row2 = read_side(ref[piece + p, rows:, :])
        parts.append(decode(ref[piece + p, :rows, :], scale))
    return jnp.concatenate(parts, axis=0), jnp.concatenate([row2[0:1], row2[1:2]], axis=1)


def remote(src, dst, send, recv, to):
    return pltpu.make_async_remote_copy(
        src_ref=src, dst_ref=dst, send_sem=send, recv_sem=recv, device_id=to,
        device_id_type=pl.DeviceIdType.MESH,
    )


class Exchange:
    def __init__(self, reverse, spans, depth, buffers, kept):
        self.reverse, self.spans, self.depth = reverse, spans, depth
        (self.sent, self.got, self.stage, self.back, self.up_out, self.up_in, self.down_out,
         self.down_in, self.a_send, self.a_recv, self.b_send, self.b_recv, self.u_send,
         self.u_recv, self.d_send, self.d_recv) = buffers
        (self.total, self.above, self.below, self.total_row, self.above_row, self.below_row) = kept
        self.plane = 2 * spans
        self.chunks, self.rows = self.back.shape[0], self.back.shape[2] - SIDE
        self.steps = self.chunks + depth - 1
        self.ctx, self.grp = lax.axis_index("ctx"), lax.axis_index("grp")
        self.level = lax.div(self.grp, 2)
        self.mine = self.ctx * 2 + lax.rem(self.grp, 2)
        self.peers = [self.peer(d) for d in range(self.plane)]
        self.places = [self.place(q) for q in self.peers]

    def peer(self, d):
        return lax.rem(self.mine + d, self.plane)

    def place(self, q):
        return (lax.div(q, 2), self.level * 2 + lax.rem(q, 2))

    def at(self, d):
        if isinstance(d, int):
            return self.peers[d], self.places[d]
        return self.peer(d), self.place(self.peer(d))

    def gather(self, g, d):
        peer, place = self.at(d)
        return remote(self.sent.at[pl.ds(peer * self.chunks + 2 * g, 2)], self.stage.at[g, self.mine],
                      self.a_send.at[g, d - 1], self.a_recv.at[g, d - 1], place)

    def scatter(self, j, d):
        peer, place = self.at(d)
        return remote(self.back.at[j, peer], self.got.at[self.mine * self.chunks + j],
                      self.b_send.at[j, d - 1], self.b_recv.at[j, d - 1], place)

    def upward(self, j):
        return remote(self.up_out.at[j], self.up_in.at[j], self.u_send.at[j], self.u_recv.at[j],
                      (self.ctx, self.grp + 2))

    def downward(self, j):
        return remote(self.down_out.at[j], self.down_in.at[j], self.d_send.at[j],
                      self.d_recv.at[j], (self.ctx, self.grp - 2))

    def load(self, ref, j, k):
        scale, row2 = read_side(ref[j, k, self.rows :, :])
        return decode(ref[j, k, : self.rows, :], scale), row2

    def staged(self, j, k):
        half, side = lax.div(j, 2), lax.rem(j, 2)
        scale, row2 = read_side(self.stage[half, k, side, self.rows :, :])
        return decode(self.stage[half, k, side, : self.rows, :], scale), row2

    def store(self, ref, j, k, state, row2):
        code, scale = encode(state)
        ref[j, k, : self.rows, :] = code
        ref[j, k, self.rows :, :] = side_rows(scale, row2)

    def chain(self, j, has_in, has_out, copy, in_buf, out_buf, kept, kept_row):
        @pl.when(has_in)
        def _():
            copy(j).wait_recv()
            for k in range(self.spans):
                kept[j, k], kept_row[j, k] = self.load(in_buf, j, k)

        @pl.when(jnp.logical_not(has_in))
        def _():
            for k in range(self.spans):
                kept[j, k] = jnp.zeros_like(kept[j, k])
                kept_row[j, k] = jnp.zeros_like(kept_row[j, k])

        @pl.when(has_out)
        def _():
            for k in range(self.spans):
                self.store(out_buf, j, k, kept[j, k] + self.total[j, k],
                           kept_row[j, k] + self.total_row[j, k])
            copy(j).start()

    def finish(self, j):
        near, near_row = (self.above, self.above_row) if self.reverse else (self.below, self.below_row)
        run = jnp.zeros(self.total.shape[2:], F32)
        run_row = jnp.zeros(self.total_row.shape[2:], F32)
        for i in range(self.spans):
            k = self.spans - 1 - i if self.reverse else i
            one, two = (2 * k + 1, 2 * k) if self.reverse else (2 * k, 2 * k + 1)
            state, row2 = run + near[j, k], run_row + near_row[j, k]
            self.store(self.back, j, one, state, row2)
            beside, beside_row = self.staged(j, one)
            self.store(self.back, j, two, state + beside, row2 + beside_row)
            run = run + self.below[j, k] + self.total[j, k] + self.above[j, k]
            run_row = run_row + self.below_row[j, k] + self.total_row[j, k] + self.above_row[j, k]
        for d in range(1, self.plane):
            self.scatter(j, d).start()
        self.got[self.mine * self.chunks + j] = self.back[j, self.mine]

    def step(self, t):
        level, depth, chunks = self.level, self.depth, self.chunks

        @pl.when((t >= 0) & (t < chunks) & (lax.rem(t, 2) == 0))
        def _():
            for d in range(1, self.plane):
                self.gather(lax.div(t, 2), d).wait_recv()

        @pl.when((t >= 0) & (t < chunks))
        def _():
            for k in range(self.spans):
                first, first_row = self.staged(t, 2 * k)
                second, second_row = self.staged(t, 2 * k + 1)
                self.total[t, k] = first + second
                self.total_row[t, k] = first_row + second_row

        j_up = t - level

        @pl.when((j_up >= 0) & (j_up < chunks))
        def _():
            self.chain(j_up, level > 0, level < depth - 1, self.upward, self.up_in,
                       self.up_out, self.below, self.below_row)

        j_down = t - (depth - 1 - level)

        @pl.when((j_down >= 0) & (j_down < chunks))
        def _():
            self.chain(j_down, level < depth - 1, level > 0, self.downward, self.down_in,
                       self.down_out, self.above, self.above_row)

        j_end = t - (depth - 1)

        @pl.when((j_end >= 0) & (j_end < chunks))
        def _():
            self.finish(j_end)

    def each_head(self, group, work):
        def one(i, unused):
            work(self.peer(i + 1) * (self.chunks // 2) + group, 2 * group, i + 1)
            return unused

        lax.fori_loop(0, self.plane, one, 0)

    def send(self, chunk, d):
        @pl.when(d < self.plane)
        def _():
            self.gather(chunk // 2, d).start()

        @pl.when(d == self.plane)
        def _():
            for i in range(2):
                self.stage[chunk // 2, self.mine, i] = self.sent[self.mine * self.chunks + chunk + i]

    def receive(self, chunk, d):
        @pl.when(d < self.plane)
        def _():
            self.scatter(chunk, self.plane - d).wait_recv()
            self.scatter(chunk + 1, self.plane - d).wait_recv()

    def drain(self):
        for j in range(self.chunks):
            for d in range(1, self.plane):
                self.scatter(j, d).wait_send()
        for g in range(self.chunks // 2):
            for d in range(1, self.plane):
                self.gather(g, d).wait_send()

        @pl.when(self.level < self.depth - 1)
        def _():
            for j in range(self.chunks):
                self.upward(j).wait_send()

        @pl.when(self.level > 0)
        def _():
            for j in range(self.chunks):
                self.downward(j).wait_send()


def kernel(spans, depth, scale, q_hbm, k_hbm, v_hbm, teacher_ref, qg_ref, kg_ref, q_ref, k_ref, v_ref, in_sem, *scratch):
    loads = [
        pltpu.make_async_copy(src, dst, in_sem.at[i])
        for i, (src, dst) in enumerate(((k_hbm, k_ref), (v_hbm, v_ref), (q_hbm, q_ref)))
    ]
    for load in loads:
        load.start()
    first, second = scratch[:22], scratch[22:44]
    (target, numer_ref, denom_ref, dn_ref, dd_ref, kl_ref, t_send, t_recv, t_own) = scratch[44:]
    prefix = Exchange(False, spans, depth, first[6:], first[:6])
    suffix = Exchange(True, spans, depth, second[6:], second[:6])
    ctx, grp, plane, groups = prefix.ctx, prefix.grp, 2 * spans, 2 * depth
    rows = q_ref.shape[0]
    feat, width = q_ref.shape[1] // H, v_ref.shape[1] // H
    per_head = feat // width
    per_group = H // groups
    heads_each = H // plane
    causal = lax.broadcasted_iota(jnp.int32, (rows, rows), 1) <= lax.broadcasted_iota(
        jnp.int32, (rows, rows), 0
    )

    def cols(head, w):
        return pl.ds(pl.multiple_of(head * w, w), w)

    def greet(to):
        pl.semaphore_signal(barrier, inc=1, device_id=to, device_id_type=pl.DeviceIdType.MESH)

    barrier = pltpu.get_barrier_semaphore()
    for d in range(1, plane):
        greet(prefix.places[d])
    for d in range(1, groups):
        greet((ctx, lax.rem(grp + d, groups)))
    pl.semaphore_wait(barrier, plane + groups - 2)

    def give(d):
        peer = lax.rem(grp + d, groups)
        return remote(teacher_ref.at[pl.ds(peer * rows, rows)], target.at[grp], t_send.at[d - 1],
                      t_recv.at[d - 1], (ctx, peer))

    own = pltpu.make_async_copy(teacher_ref.at[pl.ds(grp * rows, rows)], target.at[grp], t_own)
    own.start()
    for d in range(2, groups, 2):
        give(d).start()

    loads[0].wait()
    loads[1].wait()

    def local(head, chunk, d):
        k = k_ref[:, cols(head, feat)]
        state = dot(k, v_ref[:, cols(head, width)], TN)
        write_state(prefix.sent, head * per_head, state, jnp.sum(k.astype(F32), axis=0, keepdims=True))
        prefix.send(chunk, d)

    for group in range(heads_each):
        prefix.each_head(group, local)

    def scores_of(head):
        q, k, v = q_ref[:, cols(head, feat)], k_ref[:, cols(head, feat)], v_ref[:, cols(head, width)]
        scores = jnp.where(causal, dot(q, k, NT), 0.0)
        s_hi, s_lo = split(scores)
        numer_ref[head] = dot(s_hi, v, NN) + dot(s_lo, v, NN)
        denom_ref[head] = jnp.sum(scores, axis=1, keepdims=True)

    def forward(head, chunk, d):
        prefix.receive(chunk, d)
        q = q_ref[:, cols(head, feat)]
        q_wide = q.astype(F32)
        kv, key_row = read_state(prefix.got, head * per_head, per_head)
        kv_hi, kv_lo = split(kv)
        numer = numer_ref[head] + fold(dot(q, beside(kv_hi, kv_lo), NN))
        denom = denom_ref[head] + jnp.sum(q_wide * key_row, axis=1, keepdims=True)
        inv = 1.0 / denom
        student = numer * inv
        resid = student - target[lax.div(head, per_group), :, cols(lax.rem(head, per_group), width)].astype(F32)
        d_denom = -jnp.sum(resid * student, axis=1, keepdims=True) * inv
        dn_hi, dn_lo = split(resid * inv)
        dn = beside(dn_hi, dn_lo)
        dn_ref[head] = dn
        dd_ref[head] = d_denom
        adj = fold(dot(q, dn, TN))
        write_state(suffix.sent, head * per_head, adj, jnp.sum(d_denom * q_wide, axis=0, keepdims=True))
        suffix.send(chunk, d)

    def grads_of(head):
        q, k, v = q_ref[:, cols(head, feat)], k_ref[:, cols(head, feat)], v_ref[:, cols(head, width)]
        dn, d_denom = dn_ref[head], dd_ref[head]
        kv, key_row = read_state(prefix.got, head * per_head, per_head)
        kv_hi, kv_lo = split(kv)
        mixed = jnp.where(causal, dot(dn, beside(v, v), NT) + d_denom, 0.0)
        m_hi, m_lo = split(mixed)
        q_grad = dot(m_hi, k, NN) + dot(m_lo, k, NN)
        q_grad = q_grad + dot(dn, beside(kv_hi, kv_hi), NT) + dot(dn[:, :width], kv_lo, NT)
        q_grad = q_grad + d_denom * key_row
        qg_ref[:, cols(head, feat)] = (scale * q_grad).astype(BF16)
        kl_ref[head] = dot(m_hi, q, TN) + dot(m_lo, q, TN)

    def grads_at(i):
        grads_of(lax.rem(i, plane) * heads_each + lax.div(i, plane))

    steps, begin = prefix.steps, depth + 2
    quick, slow = 4, -(-H // (steps - 1))

    def scores_at(t):
        @pl.when(t < H // quick)
        def _():
            for i in range(quick):
                scores_of(quick * t + i)

    def step(t, unused):
        prefix.step(t)

        @pl.when(2 * t + 1 < groups)
        def _():
            give(2 * t + 1).start()

        scores_at(t + 1)
        for group in range(heads_each):

            @pl.when(t == depth + 1 + 2 * group)
            def _():
                if group == 0:
                    for d in range(1, groups):
                        give(d).wait()
                    own.wait()
                prefix.each_head(group, forward)

        suffix.step(t - begin)

        @pl.when(t >= begin)
        def _():
            for i in range(slow):
                at = slow * (t - begin) + i

                @pl.when(at < H)
                def _(at=at):
                    grads_at(at)

        return unused

    loads[2].wait()
    scores_at(0)
    lax.fori_loop(0, begin + steps, step, 0)

    def backward(head, chunk, d):
        suffix.receive(chunk, d)
        adj, row = read_state(suffix.got, head * per_head, per_head)
        a_hi, a_lo = split(adj)
        v = v_ref[:, cols(head, width)]
        k_grad = kl_ref[head] + dot(beside(v, v), beside(a_hi, a_lo), NT) + row
        kg_ref[:, cols(head, feat)] = (scale * k_grad).astype(BF16)

    for group in range(heads_each):
        suffix.each_head(group, backward)
    prefix.drain()
    suffix.drain()


def deliver_kernel(q_in, k_in, q_out, k_out):
    q_out[...] = q_in[...]
    k_out[...] = k_in[...]


def on_device(spans, groups, query_feat, key_feat, values, teacher):
    rows = query_feat.shape[0]
    feat = query_feat.shape[1] // H
    width = values.shape[1] // H
    scale = float(rows * spans * groups) ** 0.5
    depth, plane = groups // 2, 2 * spans
    pieces = H * feat // width
    chunks = pieces // plane
    length = width + SIDE
    dma = pltpu.SemaphoreType.DMA
    vmem = pl.BlockSpec(memory_space=pltpu.VMEM)
    whole = pltpu.VMEM((pieces, length, width), BF16)
    block = pltpu.VMEM((chunks, plane, length, width), BF16)
    line = pltpu.VMEM((chunks, spans, length, width), BF16)
    wide = pltpu.VMEM((chunks, spans, width, width), F32)
    row = pltpu.VMEM((chunks, spans, 2, width), F32)
    pairs = pltpu.VMEM((chunks // 2, plane, 2, length, width), BF16)
    phase = [wide] * 3 + [row] * 3 + [whole] * 2 + [pairs, block] + [line] * 4
    phase += [dma((chunks // 2, plane - 1))] * 2 + [dma((chunks, plane - 1))] * 2 + [dma((chunks,))] * 4
    column = pltpu.VMEM((H, rows, 1), F32)
    both = pltpu.VMEM((H, rows, 2 * width), BF16)
    scratch = [pltpu.VMEM(x.shape, BF16) for x in (query_feat, key_feat, values)] + [dma((3,))]
    scratch += phase + phase + [
        pltpu.VMEM((groups, rows, teacher.shape[1]), BF16),
        pltpu.VMEM((H, rows, width), F32),
        column, both, column,
        pltpu.VMEM((H, rows, feat), F32),
        dma((groups - 1,)), dma((groups - 1,)), dma,
    ]
    out = jax.ShapeDtypeStruct((rows, H * feat), BF16)
    grads = pl.pallas_call(
        functools.partial(kernel, spans, depth, scale),
        in_specs=[pl.BlockSpec(memory_space=pl.ANY)] * 4,
        out_specs=[vmem, vmem],
        out_shape=[out, out],
        scratch_shapes=scratch,
        compiler_params=pltpu.CompilerParams(
            collective_id=0, has_side_effects=True, vmem_limit_bytes=60 * 1024 * 1024
        ),
        name="grads",
    )(query_feat, key_feat, values, teacher)
    slab = pl.BlockSpec((rows // 4, H * feat), lambda i: (i, 0))
    return pl.pallas_call(
        deliver_kernel,
        grid=(4,),
        in_specs=[slab, slab],
        out_specs=[slab, slab],
        out_shape=[out, out],
        compiler_params=pltpu.CompilerParams(vmem_limit_bytes=60 * 1024 * 1024),
        name="deliver",
    )(*grads)


def solution(mesh):
    placed = (
        P(("ctx", "grp"), None),
        P(("ctx", "grp"), None),
        P(("ctx", "grp"), None),
        P("ctx", "grp"),
    )
    return jax.shard_map(
        functools.partial(on_device, mesh.shape["ctx"], mesh.shape["grp"]),
        mesh=mesh,
        in_specs=placed,
        out_specs=(P(("ctx", "grp"), None), P(("ctx", "grp"), None)),
        check_vma=False,
    )
```
